128 devices in a mesh: row: 16 (over x, z_lo, core), col: 8 (over z_hi, y).
Axes of the slice: x: 4, y: 4, z: 4 (z_hi: 2, z_lo: 2; z = z_hi * 2 + z_lo), core: 2. Of those that a mesh axis runs over, the one named last changes fastest.
Arguments:
- surface: float32 [16, 2048, 2048], P(None, 'row', 'col'), may hold values from -6 to 6
- coupling: float32 [3, 2048, 2048], P(None, 'row', 'col'), may hold values from 0.1 to 1
- w_stencil: float32 [3, 9, 16, 16], replicated, may hold values from -0.5 to 0.5
- w_patch: bfloat16 [4096, 256], replicated, may hold values from -0.09375 to 0.09375
- w_query: bfloat16 [2, 256, 256], replicated, as said below
- w_key: bfloat16 [2, 256, 256], replicated, as said below
- w_value: bfloat16 [2, 256, 256], replicated, may hold values from -0.375 to 0.375
- w_out: bfloat16 [2, 256, 256], replicated, may hold values from -4 to 4
- w_unpatch: bfloat16 [256, 4096], replicated, may hold values from -0.375 to 0.375
Outputs:
- section: float32 [16, 2048, 2048], P(None, 'row', 'col')
The draws below stay inside these ranges and needn't reach their ends.
Inputs may be any that keep to these rules, and one draw needn't show every extreme that they name: `w_key`: key projections: normal entries times 256^-0.5. `w_query`: query projections.
All inputs are finite; a program needn't handle non-finite values.
Results may differ from the reference program's by a relative error of at most 0.035.
Values may be sent and summed in bfloat16 or wider, within the bound.
A program may use at most 128 MiB of HBM per device.

```python
import math
import jax
import jax.numpy as jnp
from jax import lax

C = 16
E = 256
H = 8
PATCH = 16
LAYERS = 3
NX = 2048
NY = 2048
NPR = 128
NPC = 128
PD = 4096


def shared_normal(key):
    return jax.random.normal(jax.random.fold_in(key, 11), (2, E, E), jnp.float32)


def draw_w_key(key, part):
    key = jax.random.fold_in(key, 1)
    common = shared_normal(key)
    return (common * E ** (-0.5)).astype(jnp.bfloat16)


def draw_w_query(key, part):
    key = jax.random.fold_in(key, 2)
    own = jax.random.normal(key, (2, E, E), jnp.float32)
    mixed = own
    return (mixed * E ** (-0.5)).astype(jnp.bfloat16)


def level_of(rng, extent, cuts, least, top_value):
    def one(dim, shards_of):
        steps = jax.random.uniform(jax.random.fold_in(jax.random.fold_in(rng, 6), dim), (shards_of,), jnp.float32, least / len(cuts), top_value / len(cuts))
        return jnp.repeat(jnp.exp(steps), extent[dim] // shards_of).reshape((-1,) + (1,) * (len(extent) - dim - 1))

    level = one(*cuts[0])
    for cut in cuts[1:]:
        level = level * one(*cut)
    return level


def centred(key, shape, spread, limit, cuts=(), held_as=jnp.bfloat16):
    result = jax.random.normal(key, shape, jnp.float32) * spread
    if len(cuts) > 0:
        result = level_of(key, shape, cuts, -0.22, 0.18) * result
    return jnp.clip(result, min=-limit, max=limit).astype(held_as)


def setup_inputs(seed: int = 0) -> dict:
    seeds = jax.random.split(jax.random.key(seed), 10)
    return {
        "surface": centred(seeds[0], (C, NX, NY), 1.0, 6.0, ((1, 16), (2, 8)), jnp.float32),
        "coupling": jnp.clip(jnp.exp(math.log(1.0) - 2.3025851 * jax.random.uniform(seeds[1], (LAYERS, NX, NY), jnp.float32) ** level_of(seeds[1], (LAYERS, NX, NY), ((1, 16), (2, 8)), -0.2, 0.2)), 0.1, 1.0),
        "w_stencil": centred(seeds[2], (LAYERS, 9, C, C), (9 * C) ** -0.5, 0.5, (), jnp.float32),
        "w_patch": centred(seeds[3], (PD, E), PD ** -0.5, 0.09375),
        "w_query": draw_w_query(jax.random.fold_in(seeds[9], 71), 0),
        "w_key": draw_w_key(jax.random.fold_in(seeds[9], 71), 0),
        "w_value": centred(seeds[6], (2, E, E), E ** -0.5, 0.375),
        "w_out": centred(seeds[7], (2, E, E), (max(1, E // NPC)) ** -0.5, 4.0),
        "w_unpatch": centred(seeds[8], (E, PD), E ** -0.5, 0.375),
    }


def advance(padded, coefficient, weights):
    row_count = padded.shape[1] - 2
    col_count = padded.shape[2] - 2
    summed = jnp.zeros((padded.shape[0], row_count, col_count), jnp.float32)
    for index in range(9):
        shift_r = index // 3
        shift_c = index % 3
        summed = summed + jnp.einsum('dc,cxy->dxy', weights[index], padded[:, shift_r:shift_r + row_count, shift_c:shift_c + col_count], precision=lax.Precision.HIGHEST)
    return padded[:, 1:-1, 1:-1] + coefficient * jnp.tanh(summed)

def patchify(fine, leading, trailing):
    channels = fine.shape[0]
    return fine.reshape(channels, leading, PATCH, trailing, PATCH).transpose(1, 3, 0, 2, 4).reshape(leading * trailing, -1)

def unpatchify(detail, leading, trailing):
    return detail.reshape(leading, trailing, C, PATCH, PATCH).transpose(2, 0, 3, 1, 4).reshape(C, leading * PATCH, trailing * PATCH)

def normed(coarse):
    return (coarse * lax.rsqrt(lax.optimization_barrier(jnp.mean(coarse * coarse, axis=-1, keepdims=True)) + 1e-06)).astype(jnp.bfloat16)

def arrange(matrix, leading, trailing, layout_order):
    dims = (leading, trailing, H, E // H)
    moved = matrix.reshape(dims).transpose(layout_order)
    return moved.reshape(moved.shape[0] * moved.shape[1], moved.shape[2] * moved.shape[3])

def restore(mixed, leading, trailing, layout_order):
    dims = (leading, trailing, H, E // H)
    shaped = mixed.reshape(tuple((dims[place] for place in layout_order)))
    inverse = tuple((layout_order.index(place) for place in range(4)))
    return shaped.transpose(inverse).reshape(leading * trailing, E)

def attend(queries, lookups, values):
    head_size = E // H
    item_count = queries.shape[0]
    query_set = queries.reshape(item_count, -1, head_size).astype(jnp.float32)
    lookup_set = lookups.reshape(item_count, -1, head_size).astype(jnp.float32)
    value_set = values.reshape(item_count, -1, head_size).astype(jnp.float32)
    scores = jnp.einsum('nid,njd->nij', query_set, lookup_set) * head_size ** (-0.5)
    weights = jax.nn.softmax(scores, axis=-1).astype(jnp.bfloat16)
    mixed = jnp.einsum('nij,njd->nid', weights.astype(jnp.float32), value_set).astype(jnp.bfloat16)
    return mixed.reshape(item_count, -1)

def axial(coarse, leading, trailing, layout_order, w_q, w_k, w_v, w_o):
    normal_in = normed(coarse)
    queries = arrange(jnp.dot(normal_in, w_q, preferred_element_type=jnp.float32).astype(jnp.bfloat16), leading, trailing, layout_order)
    lookups = arrange(jnp.dot(normal_in, w_k, preferred_element_type=jnp.float32).astype(jnp.bfloat16), leading, trailing, layout_order)
    values = arrange(jnp.dot(normal_in, w_v, preferred_element_type=jnp.float32).astype(jnp.bfloat16), leading, trailing, layout_order)
    mixed = restore(attend(queries, lookups, values), leading, trailing, layout_order)
    return coarse + jnp.dot(mixed, w_o, preferred_element_type=jnp.float32)

def reference(surface, coupling, w_stencil, w_patch, w_query, w_key, w_value, w_out, w_unpatch):
    state = surface
    for layer in range(LAYERS):
        padded = jnp.pad(state, ((0, 0), (1, 1), (1, 1)))
        state = advance(padded, coupling[layer], w_stencil[layer])
    coarse = jnp.dot(patchify(state.astype(jnp.bfloat16), NPR, NPC), w_patch, preferred_element_type=jnp.float32)
    coarse = axial(coarse, NPR, NPC, (0, 2, 1, 3), w_query[0], w_key[0], w_value[0], w_out[0])
    coarse = axial(coarse, NPR, NPC, (1, 2, 0, 3), w_query[1], w_key[1], w_value[1], w_out[1])
    detail = jnp.dot(coarse.astype(jnp.bfloat16), w_unpatch, preferred_element_type=jnp.float32)
    return state + unpatchify(detail, NPR, NPC)
```

```python
import jax
import jax.numpy as jnp
from jax import lax
from jax.experimental import pallas as pl
from jax.experimental.pallas import tpu as pltpu
from jax.sharding import PartitionSpec as P

C = 16
E = 256
H = 8
PATCH = 16
LAYERS = 3
NR = 16
NC = 8
TX = 128
TY = 256
CELLS = 128
U = TX + 16
W = TY + 128
G = 14
BF = jnp.bfloat16
F32 = jnp.float32
MESH = pl.DeviceIdType.MESH
NT = (((1,), (1,)), ((), ()))
TN = (((0,), (0,)), ((), ()))

STEPS = ((-1, 0), (1, 0), (0, -1), (0, 1), (-1, -1), (-1, 1), (1, -1), (1, 1))
OPPOSITE = (1, 0, 3, 2, 7, 6, 5, 4)


def iota2(shape, dim):
    return lax.broadcasted_iota(jnp.int32, shape, dim)


def ones_where(mask):
    return jnp.where(mask, 1.0, 0.0).astype(BF)


def swap_matrix():
    row = iota2((256, 256), 0)
    col = iota2((256, 256), 1)
    return ones_where(col == (row & 15) * 16 + (row >> 4))


def mm(a, b, dims=None):
    if dims is None:
        return jnp.dot(a, b, preferred_element_type=F32)
    return lax.dot_general(a, b, dims, preferred_element_type=F32)


def strip_select(k, size, near, far):
    row = iota2((32, size), 0)
    at = iota2((32, size), 1)
    s = (row & 15) - 4 * k
    goal = jnp.where(row < 16, near, far) + s
    return ones_where((s >= 0) & (s < 3) & (at == goal))


def strip_place(k):
    return strip_select(k, 128, 125, 0)


def normed(coarse):
    mean = jnp.mean(coarse * coarse, axis=-1, keepdims=True)
    return (coarse * lax.rsqrt(mean + 1e-06)).astype(BF)


def attend(cells, w_q, w_k, w_v):
    queries = mm(cells, w_q)
    lookups = mm(cells, w_k).astype(BF)
    values = mm(cells, w_v)
    head = iota2((128, E), 1) >> 5
    query_set = jnp.concatenate(
        [jnp.where(head == h, queries, 0.0).astype(BF) for h in range(H)], axis=0
    )
    scores = mm(query_set, lookups, NT) * (E // H) ** (-0.5)
    top = jnp.max(scores, axis=-1, keepdims=True)
    powers = jnp.exp(scores - top)
    weights = (powers / jnp.sum(powers, axis=-1, keepdims=True)).astype(BF)
    mixed = jnp.zeros((128, E), F32)
    for h in range(H):
        mixed = mixed + mm(
            weights[128 * h : 128 * (h + 1)], jnp.where(head == h, values, 0.0).astype(BF)
        )
    return mixed


def main_kernel(
    surface, coupling, w_stencil, w_patch, w_query, w_key, w_value, w_out,
    state_out, coarse_out,
    surf, cp, wst, wp, wq, wqkvo, sw, am, s_ref, bb, zt,
    row_s, col_s, row_r, col_r, corner_r,
    n0, g0, mix0, m0, n1, g1, mix1, m1,
    load_sem, store_sem, halo_send, halo_recv, a2a_send, a2a_recv,
):
    row = lax.axis_index("row")
    col = lax.axis_index("col")

    loads = []

    def load(src, dst):
        copy = pltpu.make_async_copy(src, dst, load_sem.at[len(loads)])
        copy.start()
        loads.append(copy)

    for i in range(8):
        load(surface.at[:, pl.ds(16 * i, 16), :], surf.at[:, pl.ds(16 * i, 16), :])
    for l in range(LAYERS):
        load(coupling.at[l], cp.at[l, pl.ds(8, TX), pl.ds(0, TY)])
    load(w_stencil, wst)
    load(w_patch, wp)
    for n, w in enumerate((w_query, w_key, w_value, w_out)):
        load(w, wqkvo.at[n])

    row_r[...] = jnp.zeros_like(row_r)
    col_r[...] = jnp.zeros_like(col_r)
    corner_r[...] = jnp.zeros_like(corner_r)

    def has(step):
        dr, dc = step
        ok = row >= 0
        if dr < 0:
            ok = row > 0
        if dr > 0:
            ok = row < NR - 1
        if dc < 0:
            ok = ok & (col > 0)
        if dc > 0:
            ok = ok & (col < NC - 1)
        return ok

    barrier = pltpu.get_barrier_semaphore()
    for d in range(1, NC):
        pl.semaphore_signal(
            barrier, inc=1, device_id=(row, lax.rem(col + d, NC)), device_id_type=MESH
        )
    for d in range(1, NR):
        pl.semaphore_signal(
            barrier, inc=1, device_id=(lax.rem(row + d, NR), col), device_id_type=MESH
        )
    expected = jnp.int32(NC - 1 + NR - 1)
    for step in STEPS[4:]:
        @pl.when(has(step))
        def _():
            pl.semaphore_signal(
                barrier, inc=1, device_id=(row + step[0], col + step[1]), device_id_type=MESH
            )

        expected = expected + jnp.where(has(step), 1, 0)

    sw[...] = swap_matrix()

    s_ref[0:80, 0:TY] = jnp.zeros((80, TY), F32)
    s_ref[139 * 16 : U * 16, 0:TY] = jnp.zeros((80, TY), F32)
    for buf in range(2):
        bb[buf, 0:32, :] = jnp.zeros((32, W), BF)
        bb[buf, 142 * 16 : U * 16, :] = jnp.zeros((32, W), BF)
    cp[2, 0:8, :] = jnp.zeros((8, W), F32)
    cp[2, 8 + TX : U, :] = jnp.zeros((8, W), F32)
    cp[2, 8 : 8 + TX, TY:W] = jnp.zeros((TX, 128), F32)

    loads[11].wait()
    spread = ones_where((iota2((C, 256), 1) & 15) == iota2((C, 256), 0))
    tiled = mm(wst[...].astype(BF), spread)
    band = iota2((C, 256), 1) >> 4
    for l in range(LAYERS):
        for b in range(3):
            pick = [
                tiled[((l * 9 + a * 3 + b) * C) : ((l * 9 + a * 3 + b) * C) + C] for a in range(3)
            ]
            for xo in range(G):
                block = jnp.where(
                    band == xo,
                    pick[0],
                    jnp.where(
                        band == xo + 1, pick[1], jnp.where(band == xo + 2, pick[2], 0.0)
                    ),
                )
                am[l, C * xo : C * (xo + 1), 256 * b : 256 * (b + 1)] = block.astype(BF)

    for i in range(8):
        loads[i].wait()
        block = surf[:, 16 * i : 16 * (i + 1), :].reshape(256, TY)
        high = block.astype(BF)
        low = (block - high.astype(F32)).astype(BF)
        turned = mm(sw[...], high)
        rows = pl.ds((8 + 16 * i) * C, 256)
        bb[0, rows, 0:TY] = turned.astype(BF)
        s_ref[rows, 0:TY] = turned + mm(sw[...], low)

    strip = jnp.zeros((32, 512), F32)
    for k in range(4):
        strip = strip + mm(
            strip_select(k, TY, 0, TY - 3), bb[0, pl.ds((8 + 32 * k) * C, 512), 0:TY], NT
        )
    strip = strip.astype(BF)
    for l in range(LAYERS):
        loads[8 + l].wait()
    cols = jnp.zeros((32, TX), F32)
    rows_c = jnp.zeros((32, TY), F32)
    for l in range(2):
        field = cp[l, 8 : 8 + TX, 0:TY].astype(BF)
        cols = cols + mm(strip_select(l, TY, 0, TY - 3), field, NT)
        rows_c = rows_c + mm(strip_select(l, TX, 0, TX - 3), field)
    cols = cols.astype(BF)
    rows_c = rows_c.astype(BF)
    for side in range(2):
        half = slice(16 * side, 16 * (side + 1))
        col_s[side, :, 0:128] = cols[half]
        col_s[side, :, 128:640] = strip[half]
        col_s[side, :, 640:768] = cols[half]
        row_s[side, 48:64, :] = rows_c[half]
    row_s[0, 0:48, :] = bb[0, 8 * C : 11 * C, 0:TY]
    row_s[1, 0:48, :] = bb[0, (5 + TX) * C : (8 + TX) * C, 0:TY]

    pl.semaphore_wait(barrier, expected)

    lower = pl.ds(0, 256)
    upper = pl.ds(512, 256)
    pieces = (
        (row_s.at[0], row_r.at[1]),
        (row_s.at[1], row_r.at[0]),
        (col_s.at[0], col_r.at[1]),
        (col_s.at[1], col_r.at[0]),
        (col_s.at[0, :, lower], corner_r.at[3]),
        (col_s.at[1, :, lower], corner_r.at[2]),
        (col_s.at[0, :, upper], corner_r.at[1]),
        (col_s.at[1, :, upper], corner_r.at[0]),
    )

    def halo_copy(d):
        src, dst = pieces[d]
        return pltpu.make_async_remote_copy(
            src_ref=src,
            dst_ref=dst,
            send_sem=halo_send.at[d],
            recv_sem=halo_recv.at[OPPOSITE[d]],
            device_id=(row + STEPS[d][0], col + STEPS[d][1]),
            device_id_type=MESH,
        )

    for d in range(8):
        @pl.when(has(STEPS[d]))
        def _():
            halo_copy(d).start()

    loads[12].wait()
    for p in range(PATCH):
        turned = mm(sw[...], wp[:, p, :, :].reshape(256, E))
        wq[:, C * p : C * (p + 1), :] = turned.astype(BF).reshape(PATCH, C, E)
    for n in range(4):
        loads[13 + n].wait()

    for d in range(8):
        @pl.when(has(STEPS[d]))
        def _():
            halo_copy(d).wait_send()

    for d in range(8):
        @pl.when(has(STEPS[d]))
        def _():
            halo_copy(OPPOSITE[d]).wait_recv()

    for side, u, first in ((0, 5, 5), (1, 8 + TX, 0)):
        s_ref[u * C : (u + 3) * C, 0:TY] = row_r[side, 0:48, :].astype(F32)
        for l in range(2):
            at = iota2((8, 16), 0) - first
            s = iota2((8, 16), 1) - 4 * l
            pick = ones_where((at == s) & (s >= 0) & (s < 3))
            top = 0 if side == 0 else 8 + TX
            cp[l, top : top + 8, 0:TY] = mm(pick, row_r[side, 48:64, :])
    both = jnp.concatenate([col_r[0, :, 128:640], col_r[1, :, 128:640]], axis=0)
    both_c = jnp.concatenate([col_r[0, :, 0:128], col_r[1, :, 0:128]], axis=0)
    for k in range(4):
        s_ref[pl.ds((8 + 32 * k) * C, 512), TY:W] = mm(both, strip_place(k), TN)
    for l in range(2):
        cp[l, 8 : 8 + TX, TY:W] = mm(both_c, strip_place(l), TN)
    above = jnp.concatenate([corner_r[0], corner_r[1]], axis=0)
    below = jnp.concatenate([corner_r[2], corner_r[3]], axis=0)
    s_ref[0 : 8 * C, TY:W] = mm(above[:, 0:128], strip_place(3), TN)
    s_ref[(8 + TX) * C : U * C, TY:W] = mm(below[:, 128:256], strip_place(0), TN)
    for l in range(2):
        cp[l, 0:8, TY:W] = mm(above[:, 128:256], strip_place(l), TN)[TX - 8 : TX]
        cp[l, 8 + TX : U, TY:W] = mm(below[:, 0:128], strip_place(l), TN)[0:8]

    for k in range(9):
        rows = pl.ds(256 * k, 256)
        bb[0, rows, :] = s_ref[rows, :].astype(BF)

    for l in range(LAYERS):
        src, dst = l % 2, (l + 1) % 2

        def group(k, carry):
            first = pl.multiple_of((1 + G * k) * C, C)
            window = bb[src, pl.ds(first, 256), :]
            stacked = jnp.concatenate(
                [
                    jnp.concatenate([window[:, W - 1 :], window[:, : W - 1]], axis=1),
                    window,
                    jnp.concatenate([window[:, 1:], window[:, :1]], axis=1),
                ],
                axis=0,
            )
            gain = jnp.tanh(mm(am[l], stacked))
            for x in range(G):
                rows = pl.ds(pl.multiple_of(first + C * (x + 1), C), C)
                factor = cp[l, pl.ds(2 + G * k + x, 1), :]
                new = s_ref[rows, :] + factor * gain[C * x : C * (x + 1)]
                s_ref[rows, :] = new
                bb[dst, rows, :] = new.astype(BF)
            return carry

        lax.fori_loop(0, 10, group, 0)

    last = LAYERS % 2
    for i in range(8):
        block = bb[last, pl.ds((8 + 16 * i) * C, 256), 0:TY]
        zt[i] = mm(sw[...], block, NT).astype(BF)
    coarse = jnp.zeros((CELLS, E), F32)
    for q in range(PATCH):
        coarse = coarse + mm(zt[:, 16 * q : 16 * (q + 1), :].reshape(CELLS, 256), wq[q])

    def a2a(phase, src, dst, peer_slot, peer, rows, me):
        return pltpu.make_async_remote_copy(
            src_ref=src.at[pl.ds(pl.multiple_of(peer_slot * rows, rows), rows)],
            dst_ref=dst.at[pl.ds(pl.multiple_of(me * rows, rows), rows)],
            send_sem=a2a_send.at[phase, peer_slot],
            recv_sem=a2a_recv.at[phase, me],
            device_id=peer,
            device_id_type=MESH,
        )

    def exchange(phase, src, dst, axis, between=None):
        size, rows, me = (NC, 16, col) if axis == "col" else (NR, 8, row)

        def peer_of(d):
            slot = lax.rem(me + d, size)
            return slot, ((row, slot) if axis == "col" else (slot, col))

        for d in range(1, size):
            slot, peer = peer_of(d)
            a2a(phase, src, dst, slot, peer, rows, me).start()
        own = pl.ds(pl.multiple_of(me * rows, rows), rows)
        dst[own, :] = src[own, :]
        if between is not None:
            between()
        for d in range(1, size):
            slot, peer = peer_of(d)
            a2a(phase, src, dst, slot, peer, rows, me).wait_send()
            a2a(phase, src, dst, me, peer, rows, slot).wait_recv()

    def state_back():
        for i in range(8):
            block = s_ref[pl.ds((8 + 16 * i) * C, 256), 0:TY]
            high = block.astype(BF)
            low = (block - high.astype(F32)).astype(BF)
            turned = mm(sw[...], high) + mm(sw[...], low)
            surf[:, 16 * i : 16 * (i + 1), :] = turned.reshape(C, 16, TY)
        pltpu.make_async_copy(surf, state_out, store_sem).start()

    n0[...] = normed(coarse)
    exchange(0, n0, g0, "col", state_back)
    mix0[...] = attend(g0[...], wqkvo[0, 0], wqkvo[1, 0], wqkvo[2, 0]).astype(BF)
    exchange(1, mix0, m0, "col")
    coarse = coarse + mm(m0[...], wqkvo[3, 0])

    r = iota2((CELLS, CELLS), 0)
    k = iota2((CELLS, CELLS), 1)
    turn = ones_where(k == (r & 7) * 16 + (r >> 3))
    n1[...] = mm(turn, normed(coarse))
    exchange(2, n1, g1, "row")
    mix1[...] = attend(g1[...].astype(BF), wqkvo[0, 1], wqkvo[1, 1], wqkvo[2, 1])
    exchange(3, mix1, m1, "row")
    back = mm(turn, m1[...].astype(BF), TN).astype(BF)
    coarse = coarse + mm(back, wqkvo[3, 1])
    coarse_out[...] = coarse.astype(BF)
    pltpu.make_async_copy(surf, state_out, store_sem).wait()


def unpatch_kernel(coarse, w_unpatch, state, out, sw, tt):
    @pl.when(pl.program_id(0) == 0)
    def _():
        sw[...] = swap_matrix()
        turned = []
        for c in range(C):
            turned.append(mm(sw[...], w_unpatch[:, 256 * c : 256 * (c + 1)], NT).astype(BF))
        for q in range(PATCH):
            weights = jnp.concatenate([t[16 * q : 16 * (q + 1)] for t in turned], axis=0)
            cells = mm(coarse[...], weights, NT).astype(BF)
            tt[:, 16 * q : 16 * (q + 1), :] = cells.reshape(8, 16, 256)

    detail = mm(tt[pl.program_id(0)], sw[...], TN)
    out[...] = state[...] + detail.reshape(C, 16, TY)


def on_device(surface, coupling, w_stencil, w_patch, w_query, w_key, w_value, w_out, w_unpatch):
    anywhere = pl.BlockSpec(memory_space=pl.ANY)
    state, coarse = pl.pallas_call(
        main_kernel,
        out_shape=(
            jax.ShapeDtypeStruct((C, TX, TY), F32),
            jax.ShapeDtypeStruct((CELLS, E), BF),
        ),
        in_specs=[anywhere] * 8,
        out_specs=(anywhere, pl.BlockSpec(memory_space=pltpu.VMEM)),
        scratch_shapes=[
            pltpu.VMEM((C, TX, TY), F32),
            pltpu.VMEM((LAYERS, U, W), F32),
            pltpu.VMEM((LAYERS * 9 * C, C), F32),
            pltpu.VMEM((C, PATCH, PATCH, E), BF),
            pltpu.VMEM((PATCH, 256, E), BF),
            pltpu.VMEM((4, 2, E, E), BF),
            pltpu.VMEM((256, 256), BF),
            pltpu.VMEM((LAYERS, G * C, 768), BF),
            pltpu.VMEM((U * C, W), F32),
            pltpu.VMEM((2, U * C, W), BF),
            pltpu.VMEM((8, 256, 256), BF),
            pltpu.VMEM((2, 64, TY), BF),
            pltpu.VMEM((2, 16, 768), BF),
            pltpu.VMEM((2, 64, TY), BF),
            pltpu.VMEM((2, 16, 768), BF),
            pltpu.VMEM((4, 16, 256), BF),
            pltpu.VMEM((CELLS, E), BF),
            pltpu.VMEM((CELLS, E), BF),
            pltpu.VMEM((CELLS, E), BF),
            pltpu.VMEM((CELLS, E), BF),
            pltpu.VMEM((CELLS, E), F32),
            pltpu.VMEM((CELLS, E), F32),
            pltpu.VMEM((CELLS, E), F32),
            pltpu.VMEM((CELLS, E), F32),
            pltpu.SemaphoreType.DMA((17,)),
            pltpu.SemaphoreType.DMA,
            pltpu.SemaphoreType.DMA((8,)),
            pltpu.SemaphoreType.DMA((8,)),
            pltpu.SemaphoreType.DMA((4, NR)),
            pltpu.SemaphoreType.DMA((4, NR)),
        ],
        compiler_params=pltpu.CompilerParams(
            collective_id=0, has_side_effects=True, vmem_limit_bytes=48 * 1024 * 1024
        ),
    )(
        surface,
        coupling,
        w_stencil.reshape(LAYERS * 9 * C, C),
        w_patch.reshape(C, PATCH, PATCH, E),
        w_query,
        w_key,
        w_value,
        w_out,
    )
    return pl.pallas_call(
        unpatch_kernel,
        grid=(8,),
        out_shape=jax.ShapeDtypeStruct((C, TX, TY), F32),
        in_specs=[
            pl.BlockSpec((CELLS, E), lambda i: (0, 0)),
            pl.BlockSpec((E, C * 256), lambda i: (0, 0)),
            pl.BlockSpec((C, 16, TY), lambda i: (0, i, 0)),
        ],
        out_specs=pl.BlockSpec((C, 16, TY), lambda i: (0, i, 0)),
        scratch_shapes=[pltpu.VMEM((256, 256), BF), pltpu.VMEM((8, 256, 256), BF)],
        compiler_params=pltpu.CompilerParams(vmem_limit_bytes=32 * 1024 * 1024),
    )(coarse, w_unpatch, state)


def solution(mesh):
    in_specs = (P(None, "row", "col"), P(None, "row", "col"), P(), P(), P(), P(), P(), P(), P())
    out_specs = P(None, "row", "col")
    return jax.shard_map(
        on_device, mesh=mesh, in_specs=in_specs, out_specs=out_specs, check_vma=False
    )
```

```python
import jax
import jax.numpy as jnp
from jax import lax
from jax.experimental import pallas as pl
from jax.experimental.pallas import tpu as pltpu
from jax.sharding import PartitionSpec as P

C = 16
E = 256
H = 8
PATCH = 16
LAYERS = 3
NR = 16
NC = 8
TX = 128
TY = 256
CELLS = 128
U = TX + 16
W = TY + 128
G = 14
BF = jnp.bfloat16
F32 = jnp.float32
MESH = pl.DeviceIdType.MESH
NT = (((1,), (1,)), ((), ()))
TN = (((0,), (0,)), ((), ()))

STEPS = ((-1, 0), (1, 0), (0, -1), (0, 1), (-1, -1), (-1, 1), (1, -1), (1, 1))
OPPOSITE = (1, 0, 3, 2, 7, 6, 5, 4)


def iota2(shape, dim):
    return lax.broadcasted_iota(jnp.int32, shape, dim)


def ones_where(mask):
    return jnp.where(mask, 1.0, 0.0).astype(BF)


def swap_matrix():
    row = iota2((256, 256), 0)
    col = iota2((256, 256), 1)
    return ones_where(col == (row & 15) * 16 + (row >> 4))


def mm(a, b, dims=None):
    if dims is None:
        return jnp.dot(a, b, preferred_element_type=F32)
    return lax.dot_general(a, b, dims, preferred_element_type=F32)


def strip_select(k, size, near, far):
    row = iota2((32, size), 0)
    at = iota2((32, size), 1)
    s = (row & 15) - 4 * k
    goal = jnp.where(row < 16, near, far) + s
    return ones_where((s >= 0) & (s < 3) & (at == goal))


def strip_place(k):
    return strip_select(k, 128, 125, 0)


def normed(coarse):
    mean = jnp.mean(coarse * coarse, axis=-1, keepdims=True)
    return (coarse * lax.rsqrt(mean + 1e-06)).astype(BF)


def attend(cells, w_q, w_k, w_v):
    queries = mm(cells, w_q)
    lookups = mm(cells, w_k).astype(BF)
    values = mm(cells, w_v)
    head = iota2((128, E), 1) >> 5
    query_set = jnp.concatenate(
        [jnp.where(head == h, queries, 0.0).astype(BF) for h in range(H)], axis=0
    )
    scores = mm(query_set, lookups, NT) * (E // H) ** (-0.5)
    top = jnp.max(scores, axis=-1, keepdims=True)
    powers = jnp.exp(scores - top)
    weights = (powers / jnp.sum(powers, axis=-1, keepdims=True)).astype(BF)
    mixed = jnp.zeros((128, E), F32)
    for h in range(H):
        mixed = mixed + mm(
            weights[128 * h : 128 * (h + 1)], jnp.where(head == h, values, 0.0).astype(BF)
        )
    return mixed


def main_kernel(
    surface, coupling, w_stencil, w_patch, w_query, w_key, w_value, w_out, w_unpatch,
    out,
    surf, cp, wst, wp, wu, wq, wqkvo, sw, am, s_ref, bb, zt,
    row_s, col_s, row_r, col_r, corner_r,
    n0, g0, mix0, m0, n1, g1, mix1, m1,
    load_sem, store_sem, halo_send, halo_recv, a2a_send, a2a_recv,
):
    row = lax.axis_index("row")
    col = lax.axis_index("col")

    loads = []

    def load(src, dst):
        copy = pltpu.make_async_copy(src, dst, load_sem.at[len(loads)])
        copy.start()
        loads.append(copy)

    for i in range(8):
        load(surface.at[:, pl.ds(16 * i, 16), :], surf.at[:, pl.ds(16 * i, 16), :])
    for l in range(LAYERS):
        load(coupling.at[l], cp.at[l, pl.ds(8, TX), pl.ds(0, TY)])
    load(w_stencil, wst)
    load(w_patch, wp)
    for n, w in enumerate((w_query, w_key, w_value, w_out)):
        load(w, wqkvo.at[n])
    load(w_unpatch, wu)

    row_r[...] = jnp.zeros_like(row_r)
    col_r[...] = jnp.zeros_like(col_r)
    corner_r[...] = jnp.zeros_like(corner_r)

    def has(step):
        dr, dc = step
        ok = row >= 0
        if dr < 0:
            ok = row > 0
        if dr > 0:
            ok = row < NR - 1
        if dc < 0:
            ok = ok & (col > 0)
        if dc > 0:
            ok = ok & (col < NC - 1)
        return ok

    barrier = pltpu.get_barrier_semaphore()
    for d in range(1, NC):
        pl.semaphore_signal(
            barrier, inc=1, device_id=(row, lax.rem(col + d, NC)), device_id_type=MESH
        )
    for d in range(1, NR):
        pl.semaphore_signal(
            barrier, inc=1, device_id=(lax.rem(row + d, NR), col), device_id_type=MESH
        )
    expected = jnp.int32(NC - 1 + NR - 1)
    for step in STEPS[4:]:
        @pl.when(has(step))
        def _():
            pl.semaphore_signal(
                barrier, inc=1, device_id=(row + step[0], col + step[1]), device_id_type=MESH
            )

        expected = expected + jnp.where(has(step), 1, 0)

    sw[...] = swap_matrix()

    for i in range(8):
        loads[i].wait()
        block = surf[:, 16 * i : 16 * (i + 1), :].reshape(256, TY)
        high = block.astype(BF)
        low = (block - high.astype(F32)).astype(BF)
        turned = mm(sw[...], high)
        rows = pl.ds((8 + 16 * i) * C, 256)
        bb[0, rows, 0:TY] = turned.astype(BF)
        s_ref[rows, 0:TY] = turned + mm(sw[...], low)

    strip = jnp.zeros((32, 512), F32)
    for k in range(4):
        strip = strip + mm(
            strip_select(k, TY, 0, TY - 3), bb[0, pl.ds((8 + 32 * k) * C, 512), 0:TY], NT
        )
    strip = strip.astype(BF)
    for l in range(LAYERS):
        loads[8 + l].wait()
    cols = jnp.zeros((32, TX), F32)
    rows_c = jnp.zeros((32, TY), F32)
    for l in range(2):
        field = cp[l, 8 : 8 + TX, 0:TY].astype(BF)
        cols = cols + mm(strip_select(l, TY, 0, TY - 3), field, NT)
        rows_c = rows_c + mm(strip_select(l, TX, 0, TX - 3), field)
    cols = cols.astype(BF)
    rows_c = rows_c.astype(BF)
    for side in range(2):
        half = slice(16 * side, 16 * (side + 1))
        col_s[side, :, 0:128] = cols[half]
        col_s[side, :, 128:640] = strip[half]
        col_s[side, :, 640:768] = cols[half]
        row_s[side, 48:64, :] = rows_c[half]
    row_s[0, 0:48, :] = bb[0, 8 * C : 11 * C, 0:TY]
    row_s[1, 0:48, :] = bb[0, (5 + TX) * C : (8 + TX) * C, 0:TY]

    pl.semaphore_wait(barrier, expected)

    lower = pl.ds(0, 256)
    upper = pl.ds(512, 256)
    pieces = (
        (row_s.at[0], row_r.at[1]),
        (row_s.at[1], row_r.at[0]),
        (col_s.at[0], col_r.at[1]),
        (col_s.at[1], col_r.at[0]),
        (col_s.at[0, :, lower], corner_r.at[3]),
        (col_s.at[1, :, lower], corner_r.at[2]),
        (col_s.at[0, :, upper], corner_r.at[1]),
        (col_s.at[1, :, upper], corner_r.at[0]),
    )

    def halo_copy(d):
        src, dst = pieces[d]
        return pltpu.make_async_remote_copy(
            src_ref=src,
            dst_ref=dst,
            send_sem=halo_send.at[d],
            recv_sem=halo_recv.at[OPPOSITE[d]],
            device_id=(row + STEPS[d][0], col + STEPS[d][1]),
            device_id_type=MESH,
        )

    for d in range(8):
        @pl.when(has(STEPS[d]))
        def _():
            halo_copy(d).start()

    s_ref[0:80, 0:TY] = jnp.zeros((80, TY), F32)
    s_ref[139 * 16 : U * 16, 0:TY] = jnp.zeros((80, TY), F32)
    bb[0, 0:80, 0:TY] = jnp.zeros((80, TY), BF)
    bb[0, 139 * 16 : U * 16, 0:TY] = jnp.zeros((80, TY), BF)
    bb[1, 0:96, :] = jnp.zeros((96, W), BF)
    bb[1, 138 * 16 : U * 16, :] = jnp.zeros((96, W), BF)
    cp[2, 0:8, :] = jnp.zeros((8, W), F32)
    cp[2, 8 + TX : U, :] = jnp.zeros((8, W), F32)
    cp[2, 8 : 8 + TX, TY:W] = jnp.zeros((TX, 128), F32)

    loads[11].wait()
    spread = ones_where((iota2((C, 256), 1) & 15) == iota2((C, 256), 0))
    tiled = mm(wst[...].astype(BF), spread)
    band = iota2((C, 256), 1) >> 4
    for l in range(LAYERS):
        for b in range(3):
            pick = [
                tiled[((l * 9 + a * 3 + b) * C) : ((l * 9 + a * 3 + b) * C) + C] for a in range(3)
            ]
            for xo in range(G):
                block = jnp.where(
                    band == xo,
                    pick[0],
                    jnp.where(
                        band == xo + 1, pick[1], jnp.where(band == xo + 2, pick[2], 0.0)
                    ),
                )
                am[l, C * xo : C * (xo + 1), 256 * b : 256 * (b + 1)] = block.astype(BF)

    loads[12].wait()
    for p in range(PATCH):
        turned = mm(sw[...], wp[:, p, :, :].reshape(256, E))
        wq[:, C * p : C * (p + 1), :] = turned.astype(BF).reshape(PATCH, C, E)
    for n in range(4):
        loads[13 + n].wait()

    for d in range(8):
        @pl.when(has(STEPS[d]))
        def _():
            halo_copy(OPPOSITE[d]).wait_recv()

    for side, u, first in ((0, 5, 5), (1, 8 + TX, 0)):
        halo = row_r[side, 0:48, :]
        s_ref[u * C : (u + 3) * C, 0:TY] = halo.astype(F32)
        bb[0, u * C : (u + 3) * C, 0:TY] = halo
        for l in range(2):
            at = iota2((8, 16), 0) - first
            s = iota2((8, 16), 1) - 4 * l
            pick = ones_where((at == s) & (s >= 0) & (s < 3))
            top = 0 if side == 0 else 8 + TX
            cp[l, top : top + 8, 0:TY] = mm(pick, row_r[side, 48:64, :])
    def place(rows, strip, k):
        columns = mm(strip, strip_place(k), TN)
        s_ref[rows, TY:W] = columns
        bb[0, rows, TY:W] = columns.astype(BF)

    both = jnp.concatenate([col_r[0, :, 128:640], col_r[1, :, 128:640]], axis=0)
    both_c = jnp.concatenate([col_r[0, :, 0:128], col_r[1, :, 0:128]], axis=0)
    for k in range(4):
        place(pl.ds((8 + 32 * k) * C, 512), both, k)
    for l in range(2):
        cp[l, 8 : 8 + TX, TY:W] = mm(both_c, strip_place(l), TN)
    above = jnp.concatenate([corner_r[0], corner_r[1]], axis=0)
    below = jnp.concatenate([corner_r[2], corner_r[3]], axis=0)
    place(pl.ds(0, 128), above[:, 0:128], 3)
    place(pl.ds((8 + TX) * C, 128), below[:, 128:256], 0)
    for l in range(2):
        cp[l, 0:8, TY:W] = mm(above[:, 128:256], strip_place(l), TN)[TX - 8 : TX]
        cp[l, 8 + TX : U, TY:W] = mm(below[:, 0:128], strip_place(l), TN)[0:8]

    for l in range(LAYERS):
        src, dst = l % 2, (l + 1) % 2
        wide = W if l < LAYERS - 1 else TY
        for k in range(10):
            u = 6 + l + G * k
            count = G if k < 9 else 6
            depth = (count + 2) * C
            window = bb[src, (u - 1) * C : (u - 1) * C + depth, :]
            shifted = (
                jnp.concatenate([window[:, W - 1 :], window[:, : wide - 1]], axis=1),
                window[:, :wide],
                jnp.concatenate([window[:, 1:], window[:, :1]], axis=1)[:, :wide],
            )
            if count == G:
                mix = mm(am[l], jnp.concatenate(shifted, axis=0))
            else:
                mix = sum(
                    mm(am[l, 0 : count * C, 256 * b : 256 * b + depth], shifted[b])
                    for b in range(3)
                )
            gain = jnp.tanh(mix)
            for x in range(count):
                if u + x > 137 - l:
                    continue
                rows = slice((u + x) * C, (u + x + 1) * C)
                new = s_ref[rows, :wide] + cp[l, u + x : u + x + 1, :wide] * (
                    gain[C * x : C * (x + 1)]
                )
                s_ref[rows, :wide] = new
                bb[dst, rows, :wide] = new.astype(BF)

    last = LAYERS % 2
    for i in range(8):
        block = bb[last, pl.ds((8 + 16 * i) * C, 256), 0:TY]
        zt[i] = mm(sw[...], block, NT).astype(BF)
    coarse = jnp.zeros((CELLS, E), F32)
    for q in range(PATCH):
        coarse = coarse + mm(zt[:, 16 * q : 16 * (q + 1), :].reshape(CELLS, 256), wq[q])

    def a2a(phase, src, dst, peer_slot, peer, rows, me):
        return pltpu.make_async_remote_copy(
            src_ref=src.at[pl.ds(pl.multiple_of(peer_slot * rows, rows), rows)],
            dst_ref=dst.at[pl.ds(pl.multiple_of(me * rows, rows), rows)],
            send_sem=a2a_send.at[phase, peer_slot],
            recv_sem=a2a_recv.at[phase, me],
            device_id=peer,
            device_id_type=MESH,
        )

    def exchange(phase, src, dst, axis, between=None):
        size, rows, me = (NC, 16, col) if axis == "col" else (NR, 8, row)

        def peer_of(d):
            slot = lax.rem(me + d, size)
            return slot, ((row, slot) if axis == "col" else (slot, col))

        for d in range(1, size):
            slot, peer = peer_of(d)
            a2a(phase, src, dst, slot, peer, rows, me).start()
        own = pl.ds(pl.multiple_of(me * rows, rows), rows)
        dst[own, :] = src[own, :]
        if between is not None:
            between()
        for d in range(1, size):
            slot, peer = peer_of(d)
            a2a(phase, src, dst, me, peer, rows, slot).wait_recv()

        def sent():
            for d in range(1, size):
                slot, peer = peer_of(d)
                a2a(phase, src, dst, slot, peer, rows, me).wait_send()

        return sent

    def state_back():
        for i in range(8):
            block = s_ref[pl.ds((8 + 16 * i) * C, 256), 0:TY]
            high = block.astype(BF)
            low = (block - high.astype(F32)).astype(BF)
            turned = mm(sw[...], high) + mm(sw[...], low)
            surf[:, 16 * i : 16 * (i + 1), :] = turned.reshape(C, 16, TY)

    def unpatch_weights():
        loads[17].wait()
        for c in range(C):
            turned = mm(sw[...], wu[:, 256 * c : 256 * (c + 1)], NT).astype(BF)
            wq[:, C * c : C * (c + 1), :] = turned.reshape(PATCH, C, E)

    n0[...] = normed(coarse)
    sent0 = exchange(0, n0, g0, "col", state_back)
    mix0[...] = attend(g0[...], wqkvo[0, 0], wqkvo[1, 0], wqkvo[2, 0]).astype(BF)
    sent1 = exchange(1, mix0, m0, "col", unpatch_weights)
    coarse = coarse + mm(m0[...], wqkvo[3, 0])

    r = iota2((CELLS, CELLS), 0)
    k = iota2((CELLS, CELLS), 1)
    turn = ones_where(k == (r & 7) * 16 + (r >> 3))
    n1[...] = mm(turn, normed(coarse))
    sent2 = exchange(2, n1, g1, "row")
    mix1[...] = attend(g1[...].astype(BF), wqkvo[0, 1], wqkvo[1, 1], wqkvo[2, 1])
    sent3 = exchange(3, mix1, m1, "row")
    back = mm(turn, m1[...].astype(BF), TN).astype(BF)
    coarse = coarse + mm(back, wqkvo[3, 1])
    coarse = coarse.astype(BF)
    for q in range(PATCH):
        cells = mm(coarse, wq[q], NT).astype(BF)
        zt[:, 16 * q : 16 * (q + 1), :] = cells.reshape(8, 16, 256)
    stores = []
    for i in range(8):
        rows = slice(16 * i, 16 * (i + 1))
        detail = mm(zt[i], sw[...], TN)
        surf[:, rows, :] = surf[:, rows, :] + detail.reshape(C, 16, TY)
        copy = pltpu.make_async_copy(surf.at[:, rows, :], out.at[:, rows, :], store_sem.at[i])
        copy.start()
        stores.append(copy)
    for d in range(8):
        @pl.when(has(STEPS[d]))
        def _():
            halo_copy(d).wait_send()

    for sent in (sent0, sent1, sent2, sent3):
        sent()
    for copy in stores:
        copy.wait()


def on_device(surface, coupling, w_stencil, w_patch, w_query, w_key, w_value, w_out, w_unpatch):
    anywhere = pl.BlockSpec(memory_space=pl.ANY)
    return pl.pallas_call(
        main_kernel,
        out_shape=jax.ShapeDtypeStruct((C, TX, TY), F32),
        in_specs=[anywhere] * 9,
        out_specs=anywhere,
        scratch_shapes=[
            pltpu.VMEM((C, TX, TY), F32),
            pltpu.VMEM((LAYERS, U, W), F32),
            pltpu.VMEM((LAYERS * 9 * C, C), F32),
            pltpu.VMEM((C, PATCH, PATCH, E), BF),
            pltpu.VMEM((E, C * 256), BF),
            pltpu.VMEM((PATCH, 256, E), BF),
            pltpu.VMEM((4, 2, E, E), BF),
            pltpu.VMEM((256, 256), BF),
            pltpu.VMEM((LAYERS, G * C, 768), BF),
            pltpu.VMEM((U * C, W), F32),
            pltpu.VMEM((2, U * C, W), BF),
            pltpu.VMEM((8, 256, 256), BF),
            pltpu.VMEM((2, 64, TY), BF),
            pltpu.VMEM((2, 16, 768), BF),
            pltpu.VMEM((2, 64, TY), BF),
            pltpu.VMEM((2, 16, 768), BF),
            pltpu.VMEM((4, 16, 256), BF),
            pltpu.VMEM((CELLS, E), BF),
            pltpu.VMEM((CELLS, E), BF),
            pltpu.VMEM((CELLS, E), BF),
            pltpu.VMEM((CELLS, E), BF),
            pltpu.VMEM((CELLS, E), F32),
            pltpu.VMEM((CELLS, E), F32),
            pltpu.VMEM((CELLS, E), F32),
            pltpu.VMEM((CELLS, E), F32),
            pltpu.SemaphoreType.DMA((18,)),
            pltpu.SemaphoreType.DMA((8,)),
            pltpu.SemaphoreType.DMA((8,)),
            pltpu.SemaphoreType.DMA((8,)),
            pltpu.SemaphoreType.DMA((4, NR)),
            pltpu.SemaphoreType.DMA((4, NR)),
        ],
        compiler_params=pltpu.CompilerParams(
            collective_id=0, has_side_effects=True, vmem_limit_bytes=60 * 1024 * 1024
        ),
    )(
        surface,
        coupling,
        w_stencil.reshape(LAYERS * 9 * C, C),
        w_patch.reshape(C, PATCH, PATCH, E),
        w_query,
        w_key,
        w_value,
        w_out,
        w_unpatch,
    )


def solution(mesh):
    in_specs = (P(None, "row", "col"), P(None, "row", "col"), P(), P(), P(), P(), P(), P(), P())
    out_specs = P(None, "row", "col")
    return jax.shard_map(
        on_device, mesh=mesh, in_specs=in_specs, out_specs=out_specs, check_vma=False
    )
```

```python
import jax
import jax.numpy as jnp
from jax import lax
from jax.experimental import pallas as pl
from jax.experimental.pallas import tpu as pltpu
from jax.sharding import PartitionSpec as P

C = 16
E = 256
H = 8
PATCH = 16
LAYERS = 3
NR = 16
NC = 8
TX = 128
TY = 256
CELLS = 128
U = TX + 16
W = TY + 128
G = 14
BF = jnp.bfloat16
F32 = jnp.float32
MESH = pl.DeviceIdType.MESH
NT = (((1,), (1,)), ((), ()))
TN = (((0,), (0,)), ((), ()))

STEPS = ((-1, 0), (1, 0), (0, -1), (0, 1), (-1, -1), (-1, 1), (1, -1), (1, 1))
OPPOSITE = (1, 0, 3, 2, 7, 6, 5, 4)


def iota2(shape, dim):
    return lax.broadcasted_iota(jnp.int32, shape, dim)


def ones_where(mask):
    return jnp.where(mask, 1.0, 0.0).astype(BF)


def swap_matrix():
    row = iota2((256, 256), 0)
    col = iota2((256, 256), 1)
    return ones_where(col == (row & 15) * 16 + (row >> 4))


def mm(a, b, dims=None):
    if dims is None:
        return jnp.dot(a, b, preferred_element_type=F32)
    return lax.dot_general(a, b, dims, preferred_element_type=F32)


def strip_select(k, size, near, far):
    row = iota2((32, size), 0)
    at = iota2((32, size), 1)
    s = (row & 15) - 4 * k
    goal = jnp.where(row < 16, near, far) + s
    return ones_where((s >= 0) & (s < 3) & (at == goal))


def strip_place(k):
    return strip_select(k, 128, 125, 0)


def normed(coarse):
    mean = jnp.mean(coarse * coarse, axis=-1, keepdims=True)
    return (coarse * lax.rsqrt(mean + 1e-06)).astype(BF)


def attend(cells, w_q, w_k, w_v):
    queries = mm(cells, w_q)
    lookups = mm(cells, w_k).astype(BF)
    values = mm(cells, w_v)
    head = iota2((128, E), 1) >> 5
    query_set = jnp.concatenate(
        [jnp.where(head == h, queries, 0.0).astype(BF) for h in range(H)], axis=0
    )
    scores = mm(query_set, lookups, NT) * (E // H) ** (-0.5)
    top = jnp.max(scores, axis=-1, keepdims=True)
    powers = jnp.exp(scores - top)
    weights = (powers / jnp.sum(powers, axis=-1, keepdims=True)).astype(BF)
    mixed = jnp.zeros((128, E), F32)
    for h in range(H):
        mixed = mixed + mm(
            weights[128 * h : 128 * (h + 1)], jnp.where(head == h, values, 0.0).astype(BF)
        )
    return mixed


def main_kernel(
    surface, coupling, w_stencil, w_patch, w_query, w_key, w_value, w_out, w_unpatch,
    state, zt,
    surf, cp, wst, wp, wu, wq, wqkvo, sw, am, s_ref, bb,
    row_s, col_s, row_r, col_r, corner_r,
    n0, g0, mix0, m0, n1, g1, mix1, m1,
    load_sem, halo_send, halo_recv, a2a_send, a2a_recv,
):
    row = lax.axis_index("row")
    col = lax.axis_index("col")

    loads = []

    def load(src, dst):
        copy = pltpu.make_async_copy(src, dst, load_sem.at[len(loads)])
        copy.start()
        loads.append(copy)

    for i in range(8):
        load(surface.at[:, pl.ds(16 * i, 16), :], surf.at[:, pl.ds(16 * i, 16), :])
    for l in range(LAYERS):
        load(coupling.at[l], cp.at[l, pl.ds(8, TX), pl.ds(0, TY)])
    load(w_stencil, wst)
    load(w_patch, wp)
    for n, w in enumerate((w_query, w_key, w_value, w_out)):
        load(w, wqkvo.at[n])
    load(w_unpatch, wu)

    row_r[...] = jnp.zeros_like(row_r)
    col_r[...] = jnp.zeros_like(col_r)
    corner_r[...] = jnp.zeros_like(corner_r)

    def has(step):
        dr, dc = step
        ok = row >= 0
        if dr < 0:
            ok = row > 0
        if dr > 0:
            ok = row < NR - 1
        if dc < 0:
            ok = ok & (col > 0)
        if dc > 0:
            ok = ok & (col < NC - 1)
        return ok

    barrier = pltpu.get_barrier_semaphore()
    for d in range(1, NC):
        pl.semaphore_signal(
            barrier, inc=1, device_id=(row, lax.rem(col + d, NC)), device_id_type=MESH
        )
    for d in range(1, NR):
        pl.semaphore_signal(
            barrier, inc=1, device_id=(lax.rem(row + d, NR), col), device_id_type=MESH
        )
    expected = jnp.int32(NC - 1 + NR - 1)
    for step in STEPS[4:]:
        @pl.when(has(step))
        def _():
            pl.semaphore_signal(
                barrier, inc=1, device_id=(row + step[0], col + step[1]), device_id_type=MESH
            )

        expected = expected + jnp.where(has(step), 1, 0)

    sw[...] = swap_matrix()

    for i in range(8):
        loads[i].wait()
        block = surf[:, 16 * i : 16 * (i + 1), :].reshape(256, TY)
        high = block.astype(BF)
        low = (block - high.astype(F32)).astype(BF)
        turned = mm(sw[...], high)
        rows = pl.ds((8 + 16 * i) * C, 256)
        bb[0, rows, 0:TY] = turned.astype(BF)
        s_ref[rows, 0:TY] = turned + mm(sw[...], low)

    strip = jnp.zeros((32, 512), F32)
    for k in range(4):
        strip = strip + mm(
            strip_select(k, TY, 0, TY - 3), bb[0, pl.ds((8 + 32 * k) * C, 512), 0:TY], NT
        )
    strip = strip.astype(BF)
    for l in range(LAYERS):
        loads[8 + l].wait()
    cols = jnp.zeros((32, TX), F32)
    rows_c = jnp.zeros((32, TY), F32)
    for l in range(2):
        field = cp[l, 8 : 8 + TX, 0:TY].astype(BF)
        cols = cols + mm(strip_select(l, TY, 0, TY - 3), field, NT)
        rows_c = rows_c + mm(strip_select(l, TX, 0, TX - 3), field)
    cols = cols.astype(BF)
    rows_c = rows_c.astype(BF)
    for side in range(2):
        half = slice(16 * side, 16 * (side + 1))
        col_s[side, :, 0:128] = cols[half]
        col_s[side, :, 128:640] = strip[half]
        col_s[side, :, 640:768] = cols[half]
        row_s[side, 48:64, :] = rows_c[half]
    row_s[0, 0:48, :] = bb[0, 8 * C : 11 * C, 0:TY]
    row_s[1, 0:48, :] = bb[0, (5 + TX) * C : (8 + TX) * C, 0:TY]

    pl.semaphore_wait(barrier, expected)

    lower = pl.ds(0, 256)
    upper = pl.ds(512, 256)
    pieces = (
        (row_s.at[0], row_r.at[1]),
        (row_s.at[1], row_r.at[0]),
        (col_s.at[0], col_r.at[1]),
        (col_s.at[1], col_r.at[0]),
        (col_s.at[0, :, lower], corner_r.at[3]),
        (col_s.at[1, :, lower], corner_r.at[2]),
        (col_s.at[0, :, upper], corner_r.at[1]),
        (col_s.at[1, :, upper], corner_r.at[0]),
    )

    def halo_copy(d):
        src, dst = pieces[d]
        return pltpu.make_async_remote_copy(
            src_ref=src,
            dst_ref=dst,
            send_sem=halo_send.at[d],
            recv_sem=halo_recv.at[OPPOSITE[d]],
            device_id=(row + STEPS[d][0], col + STEPS[d][1]),
            device_id_type=MESH,
        )

    for d in range(8):
        @pl.when(has(STEPS[d]))
        def _():
            halo_copy(d).start()

    s_ref[0:80, 0:TY] = jnp.zeros((80, TY), F32)
    s_ref[139 * 16 : U * 16, 0:TY] = jnp.zeros((80, TY), F32)
    bb[0, 0:80, 0:TY] = jnp.zeros((80, TY), BF)
    bb[0, 139 * 16 : U * 16, 0:TY] = jnp.zeros((80, TY), BF)
    bb[1, 0:96, :] = jnp.zeros((96, W), BF)
    bb[1, 138 * 16 : U * 16, :] = jnp.zeros((96, W), BF)
    cp[2, 0:8, :] = jnp.zeros((8, W), F32)
    cp[2, 8 + TX : U, :] = jnp.zeros((8, W), F32)
    cp[2, 8 : 8 + TX, TY:W] = jnp.zeros((TX, 128), F32)

    loads[11].wait()
    spread = ones_where((iota2((C, 256), 1) & 15) == iota2((C, 256), 0))
    tiled = mm(wst[...].astype(BF), spread)
    band = iota2((C, 256), 1) >> 4
    for l in range(LAYERS):
        for b in range(3):
            pick = [
                tiled[((l * 9 + a * 3 + b) * C) : ((l * 9 + a * 3 + b) * C) + C] for a in range(3)
            ]
            for xo in range(G):
                block = jnp.where(
                    band == xo,
                    pick[0],
                    jnp.where(
                        band == xo + 1, pick[1], jnp.where(band == xo + 2, pick[2], 0.0)
                    ),
                )
                am[l, C * xo : C * (xo + 1), 256 * b : 256 * (b + 1)] = block.astype(BF)

    loads[12].wait()
    for p in range(PATCH):
        turned = mm(sw[...], wp[:, p, :, :].reshape(256, E))
        wq[:, C * p : C * (p + 1), :] = turned.astype(BF).reshape(PATCH, C, E)
    for n in range(4):
        loads[13 + n].wait()

    for d in range(8):
        @pl.when(has(STEPS[d]))
        def _():
            halo_copy(OPPOSITE[d]).wait_recv()

    for side, u, first in ((0, 5, 5), (1, 8 + TX, 0)):
        halo = row_r[side, 0:48, :]
        s_ref[u * C : (u + 3) * C, 0:TY] = halo.astype(F32)
        bb[0, u * C : (u + 3) * C, 0:TY] = halo
        for l in range(2):
            at = iota2((8, 16), 0) - first
            s = iota2((8, 16), 1) - 4 * l
            pick = ones_where((at == s) & (s >= 0) & (s < 3))
            top = 0 if side == 0 else 8 + TX
            cp[l, top : top + 8, 0:TY] = mm(pick, row_r[side, 48:64, :])
    def place(rows, strip, k):
        columns = mm(strip, strip_place(k), TN)
        s_ref[rows, TY:W] = columns
        bb[0, rows, TY:W] = columns.astype(BF)

    both = jnp.concatenate([col_r[0, :, 128:640], col_r[1, :, 128:640]], axis=0)
    both_c = jnp.concatenate([col_r[0, :, 0:128], col_r[1, :, 0:128]], axis=0)
    for k in range(4):
        place(pl.ds((8 + 32 * k) * C, 512), both, k)
    for l in range(2):
        cp[l, 8 : 8 + TX, TY:W] = mm(both_c, strip_place(l), TN)
    above = jnp.concatenate([corner_r[0], corner_r[1]], axis=0)
    below = jnp.concatenate([corner_r[2], corner_r[3]], axis=0)
    place(pl.ds(0, 128), above[:, 0:128], 3)
    place(pl.ds((8 + TX) * C, 128), below[:, 128:256], 0)
    for l in range(2):
        cp[l, 0:8, TY:W] = mm(above[:, 128:256], strip_place(l), TN)[TX - 8 : TX]
        cp[l, 8 + TX : U, TY:W] = mm(below[:, 0:128], strip_place(l), TN)[0:8]

    for l in range(LAYERS):
        src, dst = l % 2, (l + 1) % 2
        wide = W if l < LAYERS - 1 else TY
        for k in range(10):
            u = 6 + l + G * k
            count = G if k < 9 else 6
            depth = (count + 2) * C
            window = bb[src, (u - 1) * C : (u - 1) * C + depth, :]
            shifted = (
                jnp.concatenate([window[:, W - 1 :], window[:, : wide - 1]], axis=1),
                window[:, :wide],
                jnp.concatenate([window[:, 1:], window[:, :1]], axis=1)[:, :wide],
            )
            if count == G:
                mix = mm(am[l], jnp.concatenate(shifted, axis=0))
            else:
                mix = sum(
                    mm(am[l, 0 : count * C, 256 * b : 256 * b + depth], shifted[b])
                    for b in range(3)
                )
            gain = jnp.tanh(mix)
            for x in range(count):
                if u + x > 137 - l:
                    continue
                rows = slice((u + x) * C, (u + x + 1) * C)
                new = s_ref[rows, :wide] + cp[l, u + x : u + x + 1, :wide] * (
                    gain[C * x : C * (x + 1)]
                )
                s_ref[rows, :wide] = new
                bb[dst, rows, :wide] = new.astype(BF)

    last = LAYERS % 2
    for i in range(8):
        block = bb[last, pl.ds((8 + 16 * i) * C, 256), 0:TY]
        zt[i] = mm(sw[...], block, NT).astype(BF)
    coarse = jnp.zeros((CELLS, E), F32)
    for q in range(PATCH):
        coarse = coarse + mm(zt[:, 16 * q : 16 * (q + 1), :].reshape(CELLS, 256), wq[q])

    def a2a(phase, src, dst, peer_slot, peer, rows, me):
        return pltpu.make_async_remote_copy(
            src_ref=src.at[pl.ds(pl.multiple_of(peer_slot * rows, rows), rows)],
            dst_ref=dst.at[pl.ds(pl.multiple_of(me * rows, rows), rows)],
            send_sem=a2a_send.at[phase, peer_slot],
            recv_sem=a2a_recv.at[phase, me],
            device_id=peer,
            device_id_type=MESH,
        )

    def exchange(phase, src, dst, axis, between=None):
        size, rows, me = (NC, 16, col) if axis == "col" else (NR, 8, row)

        def peer_of(d):
            slot = lax.rem(me + d, size)
            return slot, ((row, slot) if axis == "col" else (slot, col))

        for d in range(1, size):
            slot, peer = peer_of(d)
            a2a(phase, src, dst, slot, peer, rows, me).start()
        own = pl.ds(pl.multiple_of(me * rows, rows), rows)
        dst[own, :] = src[own, :]
        if between is not None:
            between()
        for d in range(1, size):
            slot, peer = peer_of(d)
            a2a(phase, src, dst, me, peer, rows, slot).wait_recv()

        def sent():
            for d in range(1, size):
                slot, peer = peer_of(d)
                a2a(phase, src, dst, slot, peer, rows, me).wait_send()

        return sent

    def state_back():
        for i in range(8):
            block = s_ref[pl.ds((8 + 16 * i) * C, 256), 0:TY]
            high = block.astype(BF)
            low = (block - high.astype(F32)).astype(BF)
            turned = mm(sw[...], high) + mm(sw[...], low)
            state[:, 16 * i : 16 * (i + 1), :] = turned.reshape(C, 16, TY)

    def unpatch_weights():
        loads[17].wait()
        for c in range(C):
            turned = mm(sw[...], wu[:, 256 * c : 256 * (c + 1)], NT).astype(BF)
            wq[:, C * c : C * (c + 1), :] = turned.reshape(PATCH, C, E)

    n0[...] = normed(coarse)
    sent0 = exchange(0, n0, g0, "col", state_back)
    mix0[...] = attend(g0[...], wqkvo[0, 0], wqkvo[1, 0], wqkvo[2, 0]).astype(BF)
    sent1 = exchange(1, mix0, m0, "col", unpatch_weights)
    coarse = coarse + mm(m0[...], wqkvo[3, 0])

    r = iota2((CELLS, CELLS), 0)
    k = iota2((CELLS, CELLS), 1)
    turn = ones_where(k == (r & 7) * 16 + (r >> 3))
    n1[...] = mm(turn, normed(coarse))
    sent2 = exchange(2, n1, g1, "row")
    mix1[...] = attend(g1[...].astype(BF), wqkvo[0, 1], wqkvo[1, 1], wqkvo[2, 1])
    sent3 = exchange(3, mix1, m1, "row")
    back = mm(turn, m1[...].astype(BF), TN).astype(BF)
    coarse = coarse + mm(back, wqkvo[3, 1])
    coarse = coarse.astype(BF)
    for q in range(PATCH):
        cells = mm(coarse, wq[q], NT).astype(BF)
        zt[:, 16 * q : 16 * (q + 1), :] = cells.reshape(8, 16, 256)
    for d in range(8):
        @pl.when(has(STEPS[d]))
        def _():
            halo_copy(d).wait_send()

    for sent in (sent0, sent1, sent2, sent3):
        sent()


def add_kernel(zt, state, out, swap, held, store_sem):
    swap[...] = swap_matrix()
    stores = []
    for i in range(8):
        rows = slice(16 * i, 16 * (i + 1))
        detail = mm(zt[i], swap[...], TN)
        held[:, rows, :] = state[:, rows, :] + detail.reshape(C, 16, TY)
        copy = pltpu.make_async_copy(held.at[:, rows, :], out.at[:, rows, :], store_sem.at[i])
        copy.start()
        stores.append(copy)
    for copy in stores:
        copy.wait()


def on_device(surface, coupling, w_stencil, w_patch, w_query, w_key, w_value, w_out, w_unpatch):
    anywhere = pl.BlockSpec(memory_space=pl.ANY)
    in_vmem = pl.BlockSpec(memory_space=pltpu.VMEM)
    state, cells = pl.pallas_call(
        main_kernel,
        out_shape=(pltpu.VMEM((C, TX, TY), F32), pltpu.VMEM((8, 256, 256), BF)),
        in_specs=[anywhere] * 9,
        out_specs=(in_vmem, in_vmem),
        scratch_shapes=[
            pltpu.VMEM((C, TX, TY), F32),
            pltpu.VMEM((LAYERS, U, W), F32),
            pltpu.VMEM((LAYERS * 9 * C, C), F32),
            pltpu.VMEM((C, PATCH, PATCH, E), BF),
            pltpu.VMEM((E, C * 256), BF),
            pltpu.VMEM((PATCH, 256, E), BF),
            pltpu.VMEM((4, 2, E, E), BF),
            pltpu.VMEM((256, 256), BF),
            pltpu.VMEM((LAYERS, G * C, 768), BF),
            pltpu.VMEM((U * C, W), F32),
            pltpu.VMEM((2, U * C, W), BF),
            pltpu.VMEM((2, 64, TY), BF),
            pltpu.VMEM((2, 16, 768), BF),
            pltpu.VMEM((2, 64, TY), BF),
            pltpu.VMEM((2, 16, 768), BF),
            pltpu.VMEM((4, 16, 256), BF),
            pltpu.VMEM((CELLS, E), BF),
            pltpu.VMEM((CELLS, E), BF),
            pltpu.VMEM((CELLS, E), BF),
            pltpu.VMEM((CELLS, E), BF),
            pltpu.VMEM((CELLS, E), F32),
            pltpu.VMEM((CELLS, E), F32),
            pltpu.VMEM((CELLS, E), F32),
            pltpu.VMEM((CELLS, E), F32),
            pltpu.SemaphoreType.DMA((18,)),
            pltpu.SemaphoreType.DMA((8,)),
            pltpu.SemaphoreType.DMA((8,)),
            pltpu.SemaphoreType.DMA((4, NR)),
            pltpu.SemaphoreType.DMA((4, NR)),
        ],
        compiler_params=pltpu.CompilerParams(
            collective_id=0, has_side_effects=True, vmem_limit_bytes=60 * 1024 * 1024
        ),
    )(
        surface,
        coupling,
        w_stencil.reshape(LAYERS * 9 * C, C),
        w_patch.reshape(C, PATCH, PATCH, E),
        w_query,
        w_key,
        w_value,
        w_out,
        w_unpatch,
    )
    return pl.pallas_call(
        add_kernel,
        out_shape=jax.ShapeDtypeStruct((C, TX, TY), F32),
        in_specs=[in_vmem, in_vmem],
        out_specs=anywhere,
        scratch_shapes=[
            pltpu.VMEM((256, 256), BF),
            pltpu.VMEM((C, TX, TY), F32),
            pltpu.SemaphoreType.DMA((8,)),
        ],
        compiler_params=pltpu.CompilerParams(vmem_limit_bytes=32 * 1024 * 1024),
    )(cells, state)


def solution(mesh):
    in_specs = (P(None, "row", "col"), P(None, "row", "col"), P(), P(), P(), P(), P(), P(), P())
    out_specs = P(None, "row", "col")
    return jax.shard_map(
        on_device, mesh=mesh, in_specs=in_specs, out_specs=out_specs, check_vma=False
    )
```

```python
import jax
import jax.numpy as jnp
from jax import lax
from jax.experimental import pallas as pl
from jax.experimental.pallas import tpu as pltpu
from jax.sharding import PartitionSpec as P

C = 16
E = 256
H = 8
PATCH = 16
LAYERS = 3
NR = 16
NC = 8
TX = 128
TY = 256
CELLS = 128
U = TX + 16
W = TY + 128
G = 6
DEPTH = (G + 2) * C
BF = jnp.bfloat16
F32 = jnp.float32
MESH = pl.DeviceIdType.MESH
NT = (((1,), (1,)), ((), ()))
TN = (((0,), (0,)), ((), ()))

STEPS = ((-1, 0), (1, 0), (0, -1), (0, 1), (-1, -1), (-1, 1), (1, -1), (1, 1))
OPPOSITE = (1, 0, 3, 2, 7, 6, 5, 4)
ROW_ORDER = (10, 6, 9, 7, 8, 11, 5, 12, 4, 13, 3, 14, 2, 15, 1)
COL_ORDER = (6, 2, 5, 3, 4, 7, 1)


def iota2(shape, dim):
    return lax.broadcasted_iota(jnp.int32, shape, dim)


def ones_where(mask):
    return jnp.where(mask, 1.0, 0.0).astype(BF)


def swap_matrix():
    row = iota2((256, 256), 0)
    col = iota2((256, 256), 1)
    return ones_where(col == (row & 15) * 16 + (row >> 4))


def mm(a, b, dims=None):
    if dims is None:
        return jnp.dot(a, b, preferred_element_type=F32)
    return lax.dot_general(a, b, dims, preferred_element_type=F32)


def strip_select(k, size, near, far):
    row = iota2((32, size), 0)
    at = iota2((32, size), 1)
    s = (row & 15) - 4 * k
    goal = jnp.where(row < 16, near, far) + s
    return ones_where((s >= 0) & (s < 3) & (at == goal))


def strip_place(k):
    return strip_select(k, 128, 125, 0)


def normed(coarse):
    mean = jnp.mean(coarse * coarse, axis=-1, keepdims=True)
    return (coarse * lax.rsqrt(mean + 1e-06)).astype(BF)


def softmax(scores):
    scores = scores * (E // H) ** (-0.5)
    top = jnp.max(scores, axis=-1, keepdims=True)
    powers = jnp.exp(scores - top)
    return (powers / jnp.sum(powers, axis=-1, keepdims=True)).astype(BF)


def packed(cells):
    parts = cells.reshape(16, 8, E)
    return (
        jnp.stack([parts[:, :, :128], parts[:, :, 128:]], axis=1).reshape(256, 128).astype(BF)
    )


def unpacked(rows):
    parts = rows.astype(F32).reshape(16, 2, 8, 128)
    return jnp.concatenate([parts[:, 0], parts[:, 1]], axis=-1).reshape(CELLS, E)


def attend(cells, w_q, w_k, w_v):
    queries = mm(cells, w_q)
    lookups = mm(cells, w_k).astype(BF)
    values = mm(cells, w_v)
    head = iota2((128, E), 1) >> 5
    query_set = jnp.concatenate(
        [jnp.where(head == h, queries, 0.0).astype(BF) for h in range(H)], axis=0
    )
    weights = softmax(mm(query_set, lookups, NT))
    mixed = jnp.zeros((128, E), F32)
    for h in range(H):
        mixed = mixed + mm(
            weights[128 * h : 128 * (h + 1)], jnp.where(head == h, values, 0.0).astype(BF)
        )
    return mixed


def main_kernel(
    surface, coupling, w_stencil, w_patch, w_query, w_key, w_value, w_out, w_unpatch,
    state, zt,
    surf, cp, wst, wp, wu, wq, wqkvo, sw, am, s_ref, bb,
    row_s, col_s, row_r, col_r, corner_r,
    g0, k0, v0, n1, g1, mix1, m1,
    load_sem, halo_send, halo_recv, gather_send, gather_recv, a2a_send, a2a_recv,
):
    row = lax.axis_index("row")
    col = lax.axis_index("col")

    row_r[...] = jnp.zeros_like(row_r)
    col_r[...] = jnp.zeros_like(col_r)
    corner_r[...] = jnp.zeros_like(corner_r)

    def has(step):
        dr, dc = step
        ok = row >= 0
        if dr < 0:
            ok = row > 0
        if dr > 0:
            ok = row < NR - 1
        if dc < 0:
            ok = ok & (col > 0)
        if dc > 0:
            ok = ok & (col < NC - 1)
        return ok

    barrier = pltpu.get_barrier_semaphore()
    for d in range(1, NC):
        pl.semaphore_signal(
            barrier, inc=1, device_id=(row, lax.rem(col + d, NC)), device_id_type=MESH
        )
    for d in range(1, NR):
        pl.semaphore_signal(
            barrier, inc=1, device_id=(lax.rem(row + d, NR), col), device_id_type=MESH
        )
    expected = jnp.int32(NC - 1 + NR - 1)
    for step in STEPS[4:]:
        @pl.when(has(step))
        def _():
            pl.semaphore_signal(
                barrier, inc=1, device_id=(row + step[0], col + step[1]), device_id_type=MESH
            )

        expected = expected + jnp.where(has(step), 1, 0)

    loads = []

    def load(src, dst):
        copy = pltpu.make_async_copy(src, dst, load_sem.at[len(loads)])
        copy.start()
        loads.append(copy)

    for i in range(8):
        load(surface.at[:, pl.ds(16 * i, 16), :], surf.at[:, pl.ds(16 * i, 16), :])
    for l in range(LAYERS):
        load(coupling.at[l], cp.at[l, pl.ds(8, TX), pl.ds(0, TY)])
    load(w_stencil, wst)
    load(w_patch, wp)
    for n, w in enumerate((w_query, w_key, w_value, w_out)):
        load(w, wqkvo.at[n])
    load(w_unpatch, wu)

    sw[...] = swap_matrix()

    for i in range(8):
        loads[i].wait()
        high = surf[:, 16 * i : 16 * (i + 1), :].reshape(256, TY).astype(BF)
        bb[0, pl.ds((8 + 16 * i) * C, 256), 0:TY] = mm(sw[...], high).astype(BF)

    strip = jnp.zeros((32, 512), F32)
    for k in range(4):
        strip = strip + mm(
            strip_select(k, TY, 0, TY - 3), bb[0, pl.ds((8 + 32 * k) * C, 512), 0:TY], NT
        )
    strip = strip.astype(BF)
    for l in range(2):
        loads[8 + l].wait()
    cols = jnp.zeros((32, TX), F32)
    rows_c = jnp.zeros((32, TY), F32)
    for l in range(2):
        field = cp[l, 8 : 8 + TX, 0:TY].astype(BF)
        cols = cols + mm(strip_select(l, TY, 0, TY - 3), field, NT)
        rows_c = rows_c + mm(strip_select(l, TX, 0, TX - 3), field)
    cols = cols.astype(BF)
    rows_c = rows_c.astype(BF)
    for side in range(2):
        half = slice(16 * side, 16 * (side + 1))
        col_s[side, :, 0:128] = cols[half]
        col_s[side, :, 128:640] = strip[half]
        col_s[side, :, 640:768] = cols[half]
        row_s[side, 48:64, :] = rows_c[half]
    row_s[0, 0:48, :] = bb[0, 8 * C : 11 * C, 0:TY]
    row_s[1, 0:48, :] = bb[0, (5 + TX) * C : (8 + TX) * C, 0:TY]

    pl.semaphore_wait(barrier, expected)

    lower = pl.ds(0, 256)
    upper = pl.ds(512, 256)
    pieces = (
        (row_s.at[0], row_r.at[1]),
        (row_s.at[1], row_r.at[0]),
        (col_s.at[0], col_r.at[1]),
        (col_s.at[1], col_r.at[0]),
        (col_s.at[0, :, lower], corner_r.at[3]),
        (col_s.at[1, :, lower], corner_r.at[2]),
        (col_s.at[0, :, upper], corner_r.at[1]),
        (col_s.at[1, :, upper], corner_r.at[0]),
    )

    def halo_copy(d):
        src, dst = pieces[d]
        return pltpu.make_async_remote_copy(
            src_ref=src,
            dst_ref=dst,
            send_sem=halo_send.at[d],
            recv_sem=halo_recv.at[OPPOSITE[d]],
            device_id=(row + STEPS[d][0], col + STEPS[d][1]),
            device_id_type=MESH,
        )

    for d in (4, 5, 6, 7, 2, 3, 0, 1):
        @pl.when(has(STEPS[d]))
        def _():
            halo_copy(d).start()

    for i in range(8):
        block = surf[:, 16 * i : 16 * (i + 1), :].reshape(256, TY)
        low = (block - block.astype(BF).astype(F32)).astype(BF)
        rows = pl.ds((8 + 16 * i) * C, 256)
        s_ref[rows, 0:TY] = bb[0, rows, 0:TY].astype(F32) + mm(sw[...], low)

    s_ref[0:80, 0:TY] = jnp.zeros((80, TY), F32)
    s_ref[139 * 16 : U * 16, 0:TY] = jnp.zeros((80, TY), F32)
    bb[0, 0:80, 0:TY] = jnp.zeros((80, TY), BF)
    bb[0, 139 * 16 : U * 16, 0:TY] = jnp.zeros((80, TY), BF)
    bb[1, 0:96, :] = jnp.zeros((96, W), BF)
    bb[1, 138 * 16 : U * 16, :] = jnp.zeros((96, W), BF)
    cp[2, 0:8, :] = jnp.zeros((8, W), F32)
    cp[2, 8 + TX : U, :] = jnp.zeros((8, W), F32)
    cp[2, 8 : 8 + TX, TY:W] = jnp.zeros((TX, 128), F32)

    loads[10].wait()
    loads[11].wait()
    spread = ones_where((iota2((C, DEPTH), 1) & 15) == iota2((C, DEPTH), 0))
    tiled = mm(wst[...].astype(BF), spread)
    band = iota2((C, DEPTH), 1) >> 4
    for l in range(LAYERS):
        for b in range(3):
            pick = [
                tiled[((l * 9 + a * 3 + b) * C) : ((l * 9 + a * 3 + b) * C) + C] for a in range(3)
            ]
            for xo in range(G):
                block = jnp.where(
                    band == xo,
                    pick[0],
                    jnp.where(
                        band == xo + 1, pick[1], jnp.where(band == xo + 2, pick[2], 0.0)
                    ),
                )
                am[l, C * xo : C * (xo + 1), DEPTH * b : DEPTH * (b + 1)] = block.astype(BF)

    loads[12].wait()
    for p in range(PATCH):
        turned = mm(sw[...], wp[:, p, :, :].reshape(256, E))
        wq[:, C * p : C * (p + 1), :] = turned.astype(BF).reshape(PATCH, C, E)
    for n in range(4):
        loads[13 + n].wait()

    for d in range(8):
        @pl.when(has(STEPS[d]))
        def _():
            halo_copy(OPPOSITE[d]).wait_recv()

    for side, u, first in ((0, 5, 5), (1, 8 + TX, 0)):
        halo = row_r[side, 0:48, :]
        s_ref[u * C : (u + 3) * C, 0:TY] = halo.astype(F32)
        bb[0, u * C : (u + 3) * C, 0:TY] = halo
        for l in range(2):
            at = iota2((8, 16), 0) - first
            s = iota2((8, 16), 1) - 4 * l
            pick = ones_where((at == s) & (s >= 0) & (s < 3))
            top = 0 if side == 0 else 8 + TX
            cp[l, top : top + 8, 0:TY] = mm(pick, row_r[side, 48:64, :])
    def place(rows, strip, k):
        columns = mm(strip, strip_place(k), TN)
        s_ref[rows, TY:W] = columns
        bb[0, rows, TY:W] = columns.astype(BF)

    both = jnp.concatenate([col_r[0, :, 128:640], col_r[1, :, 128:640]], axis=0)
    both_c = jnp.concatenate([col_r[0, :, 0:128], col_r[1, :, 0:128]], axis=0)
    for k in range(4):
        place(pl.ds((8 + 32 * k) * C, 512), both, k)
    for l in range(2):
        cp[l, 8 : 8 + TX, TY:W] = mm(both_c, strip_place(l), TN)
    above = jnp.concatenate([corner_r[0], corner_r[1]], axis=0)
    below = jnp.concatenate([corner_r[2], corner_r[3]], axis=0)
    place(pl.ds(0, 128), above[:, 0:128], 3)
    place(pl.ds((8 + TX) * C, 128), below[:, 128:256], 0)
    for l in range(2):
        cp[l, 0:8, TY:W] = mm(above[:, 128:256], strip_place(l), TN)[TX - 8 : TX]
        cp[l, 8 + TX : U, TY:W] = mm(below[:, 0:128], strip_place(l), TN)[0:8]

    for l in range(LAYERS):
        src, dst = l % 2, (l + 1) % 2

        def shifted(u):
            window = bb[src, (u - 1) * C : (u - 1) * C + DEPTH, :]
            return jnp.concatenate(
                [
                    jnp.concatenate([window[:, W - 1 :], window[:, : W - 1]], axis=1),
                    window,
                    jnp.concatenate([window[:, 1:], window[:, :1]], axis=1),
                ],
                axis=0,
            )

        def update(u, gain, lanes):
            for x in range(G):
                if u + x > 137 - l:
                    continue
                rows = slice((u + x) * C, (u + x + 1) * C)
                new = s_ref[rows, lanes] + cp[l, u + x : u + x + 1, lanes] * (
                    gain[C * x : C * (x + 1)]
                )
                s_ref[rows, lanes] = new
                bb[dst, rows, lanes] = new.astype(BF)

        for pair in range(11):
            starts = [6 + l + G * (2 * pair + n) for n in range(2)]
            windows = [shifted(u) for u in starts]
            for u, window in zip(starts, windows):
                update(u, jnp.tanh(mm(am[l], window[:, :TY])), slice(0, TY))
            if l < LAYERS - 1:
                edges = jnp.tanh(
                    mm(am[l], jnp.concatenate([window[:, TY:] for window in windows], axis=1))
                )
                for n, u in enumerate(starts):
                    update(u, edges[:, 128 * n : 128 * (n + 1)], slice(TY, W))

    last = LAYERS % 2
    for i in range(8):
        block = bb[last, pl.ds((8 + 16 * i) * C, 256), 0:TY]
        zt[i] = mm(sw[...], block, NT).astype(BF)
    coarse = jnp.zeros((CELLS, E), F32)
    for q in range(PATCH):
        coarse = coarse + mm(zt[:, 16 * q : 16 * (q + 1), :].reshape(CELLS, 256), wq[q])

    def a2a(phase, src, dst, d):
        rows = pl.ds(16 * d, 16)
        return pltpu.make_async_remote_copy(
            src_ref=src.at[rows],
            dst_ref=dst.at[rows],
            send_sem=a2a_send.at[phase, d],
            recv_sem=a2a_recv.at[phase],
            device_id=(lax.rem(row + (d if phase == 0 else NR - d), NR), col),
            device_id_type=MESH,
        )

    def exchange(phase, src, dst):
        for d in ROW_ORDER:
            a2a(phase, src, dst, d).start()
        dst[0:16, :] = src[0:16, :]
        rest = pl.ds(16, 16 * (NR - 1))
        pltpu.make_async_remote_copy(
            src_ref=src.at[rest],
            dst_ref=dst.at[rest],
            send_sem=a2a_send.at[phase, 1],
            recv_sem=a2a_recv.at[phase],
            device_id=(lax.rem(row + 1, NR), col),
            device_id_type=MESH,
        ).wait_recv()

    def gather(d):
        return pltpu.make_async_remote_copy(
            src_ref=g0.at[0],
            dst_ref=g0.at[d],
            send_sem=gather_send.at[d],
            recv_sem=gather_recv.at[d],
            device_id=(row, lax.rem(col + d, NC)),
            device_id_type=MESH,
        )

    def state_back():
        for i in range(8):
            block = s_ref[pl.ds((8 + 16 * i) * C, 256), 0:TY]
            high = block.astype(BF)
            low = (block - high.astype(F32)).astype(BF)
            turned = mm(sw[...], high) + mm(sw[...], low)
            state[:, 16 * i : 16 * (i + 1), :] = turned.reshape(C, 16, TY)

    def unpatch_weights():
        loads[17].wait()
        for c in range(C):
            turned = mm(sw[...], wu[:, 256 * c : 256 * (c + 1)], NT).astype(BF)
            wq[:, C * c : C * (c + 1), :] = turned.reshape(PATCH, C, E)

    g0[0] = normed(coarse)
    for d in COL_ORDER:
        gather(d).start()
    head = iota2((16, E), 1) >> 5
    queries = mm(g0[0], wqkvo[0, 0])
    query_sets = [
        jnp.concatenate(
            [
                jnp.where(head == h, queries[16 * i : 16 * (i + 1)], 0.0).astype(BF)
                for h in range(H)
            ],
            axis=0,
        )
        for i in range(8)
    ]
    state_back()
    unpatch_weights()
    for d in range(NC):
        if d > 0:
            gather(d).wait_recv()
        k0[d] = mm(g0[d], wqkvo[1, 0]).astype(BF)
        v0[d] = mm(g0[d], wqkvo[2, 0]).astype(BF)
    mixed = []
    for i in range(8):
        rows = slice(16 * i, 16 * (i + 1))
        weights = softmax(mm(query_sets[i], k0[:, rows, :].reshape(128, E), NT))
        whole = mm(weights, v0[:, rows, :].reshape(128, E))
        mixed.append(
            sum(jnp.where(head == h, whole[16 * h : 16 * (h + 1)], 0.0) for h in range(H))
        )
    coarse = coarse + mm(jnp.concatenate(mixed, axis=0).astype(BF), wqkvo[3, 0])

    r = iota2((CELLS, CELLS), 0)
    k = iota2((CELLS, CELLS), 1)
    turn = ones_where(k == (r & 7) * 16 + (((r >> 3) + row) & 15))
    n1[...] = packed(mm(turn, normed(coarse)))
    exchange(0, n1, g1)
    mix1[...] = packed(
        attend(unpacked(g1[...]).astype(BF), wqkvo[0, 1], wqkvo[1, 1], wqkvo[2, 1])
    )
    exchange(1, mix1, m1)
    back = mm(turn, unpacked(m1[...]).astype(BF), TN).astype(BF)
    coarse = coarse + mm(back, wqkvo[3, 1])
    coarse = coarse.astype(BF)
    for q in range(PATCH):
        cells = mm(coarse, wq[q], NT).astype(BF)
        zt[:, 16 * q : 16 * (q + 1), :] = cells.reshape(8, 16, 256)
    for d in range(8):
        @pl.when(has(STEPS[d]))
        def _():
            halo_copy(d).wait_send()

    for d in COL_ORDER:
        gather(d).wait_send()
    for d in ROW_ORDER:
        a2a(0, n1, g1, d).wait_send()
        a2a(1, mix1, m1, d).wait_send()


def add_kernel(zt, state, out, swap, held, store_sem):
    swap[...] = swap_matrix()
    stores = []
    for i in range(8):
        rows = slice(16 * i, 16 * (i + 1))
        detail = mm(zt[i], swap[...], TN)
        held[:, rows, :] = state[:, rows, :] + detail.reshape(C, 16, TY)
        copy = pltpu.make_async_copy(held.at[:, rows, :], out.at[:, rows, :], store_sem.at[i])
        copy.start()
        stores.append(copy)
    for copy in stores:
        copy.wait()


def on_device(surface, coupling, w_stencil, w_patch, w_query, w_key, w_value, w_out, w_unpatch):
    anywhere = pl.BlockSpec(memory_space=pl.ANY)
    in_vmem = pl.BlockSpec(memory_space=pltpu.VMEM)
    state, cells = pl.pallas_call(
        main_kernel,
        out_shape=(pltpu.VMEM((C, TX, TY), F32), pltpu.VMEM((8, 256, 256), BF)),
        in_specs=[anywhere] * 9,
        out_specs=(in_vmem, in_vmem),
        scratch_shapes=[
            pltpu.VMEM((C, TX, TY), F32),
            pltpu.VMEM((LAYERS, U, W), F32),
            pltpu.VMEM((LAYERS * 9 * C, C), F32),
            pltpu.VMEM((C, PATCH, PATCH, E), BF),
            pltpu.VMEM((E, C * 256), BF),
            pltpu.VMEM((PATCH, 256, E), BF),
            pltpu.VMEM((4, 2, E, E), BF),
            pltpu.VMEM((256, 256), BF),
            pltpu.VMEM((LAYERS, G * C, 3 * DEPTH), BF),
            pltpu.VMEM((U * C, W), F32),
            pltpu.VMEM((2, U * C, W), BF),
            pltpu.VMEM((2, 64, TY), BF),
            pltpu.VMEM((2, 16, 768), BF),
            pltpu.VMEM((2, 64, TY), BF),
            pltpu.VMEM((2, 16, 768), BF),
            pltpu.VMEM((4, 16, 256), BF),
            pltpu.VMEM((NC, CELLS, E), BF),
            pltpu.VMEM((NC, CELLS, E), BF),
            pltpu.VMEM((NC, CELLS, E), BF),
            pltpu.VMEM((256, 128), BF),
            pltpu.VMEM((256, 128), BF),
            pltpu.VMEM((256, 128), BF),
            pltpu.VMEM((256, 128), BF),
            pltpu.SemaphoreType.DMA((18,)),
            pltpu.SemaphoreType.DMA((8,)),
            pltpu.SemaphoreType.DMA((8,)),
            pltpu.SemaphoreType.DMA((NC,)),
            pltpu.SemaphoreType.DMA((NC,)),
            pltpu.SemaphoreType.DMA((2, NR)),
            pltpu.SemaphoreType.DMA((2,)),
        ],
        compiler_params=pltpu.CompilerParams(
            collective_id=0, has_side_effects=True, vmem_limit_bytes=60 * 1024 * 1024
        ),
    )(
        surface,
        coupling,
        w_stencil.reshape(LAYERS * 9 * C, C),
        w_patch.reshape(C, PATCH, PATCH, E),
        w_query,
        w_key,
        w_value,
        w_out,
        w_unpatch,
    )
    return pl.pallas_call(
        add_kernel,
        out_shape=jax.ShapeDtypeStruct((C, TX, TY), F32),
        in_specs=[in_vmem, in_vmem],
        out_specs=anywhere,
        scratch_shapes=[
            pltpu.VMEM((256, 256), BF),
            pltpu.VMEM((C, TX, TY), F32),
            pltpu.SemaphoreType.DMA((8,)),
        ],
        compiler_params=pltpu.CompilerParams(vmem_limit_bytes=32 * 1024 * 1024),
    )(cells, state)


def solution(mesh):
    in_specs = (P(None, "row", "col"), P(None, "row", "col"), P(), P(), P(), P(), P(), P(), P())
    out_specs = P(None, "row", "col")
    return jax.shard_map(
        on_device, mesh=mesh, in_specs=in_specs, out_specs=out_specs, check_vma=False
    )
```

```python
import jax
import jax.numpy as jnp
from jax import lax
from jax.experimental import pallas as pl
from jax.experimental.pallas import tpu as pltpu
from jax.sharding import PartitionSpec as P

C = 16
E = 256
H = 8
PATCH = 16
LAYERS = 3
NR = 16
NC = 8
TX = 128
TY = 256
CELLS = 128
U = TX + 16
W = TY + 128
G = 6
DEPTH = (G + 2) * C
BF = jnp.bfloat16
F32 = jnp.float32
MESH = pl.DeviceIdType.MESH
NT = (((1,), (1,)), ((), ()))
TN = (((0,), (0,)), ((), ()))

STEPS = ((-1, 0), (1, 0), (0, -1), (0, 1), (-1, -1), (-1, 1), (1, -1), (1, 1))
OPPOSITE = (1, 0, 3, 2, 7, 6, 5, 4)
ROW_ORDER = (10, 11, 8, 9, 14, 15, 12, 13, 6, 7, 4, 5, 2, 3, 1)
COL_ORDER = (6, 5, 7, 2, 4, 1, 3)
GATHER_ORDER = (2, 1, 3, 4, 6, 5, 7)


def iota2(shape, dim):
    return lax.broadcasted_iota(jnp.int32, shape, dim)


def ones_where(mask):
    return jnp.where(mask, 1.0, 0.0).astype(BF)


def swap_matrix():
    row = iota2((256, 256), 0)
    col = iota2((256, 256), 1)
    return ones_where(col == (row & 15) * 16 + (row >> 4))


def mm(a, b, dims=None):
    if dims is None:
        return jnp.dot(a, b, preferred_element_type=F32)
    return lax.dot_general(a, b, dims, preferred_element_type=F32)


def strip_select(k, size, near, far):
    row = iota2((32, size), 0)
    at = iota2((32, size), 1)
    s = (row & 15) - 4 * k
    goal = jnp.where(row < 16, near, far) + s
    return ones_where((s >= 0) & (s < 3) & (at == goal))


def strip_place(k):
    return strip_select(k, 128, 125, 0)


def normed(coarse):
    mean = jnp.mean(coarse * coarse, axis=-1, keepdims=True)
    return (coarse * lax.rsqrt(mean + 1e-06)).astype(BF)


def softmax(scores):
    scores = scores * (E // H) ** (-0.5)
    top = jnp.max(scores, axis=-1, keepdims=True)
    powers = jnp.exp(scores - top)
    return (powers / jnp.sum(powers, axis=-1, keepdims=True)).astype(BF)


def flipped(bits, d):
    return sum(((1 - bit) if (d >> n) & 1 else bit) * (1 << n) for n, bit in enumerate(bits))


def packed(cells):
    parts = cells.reshape(16, 8, E)
    return (
        jnp.stack([parts[:, :, :128], parts[:, :, 128:]], axis=1).reshape(256, 128).astype(BF)
    )


def unpacked(rows):
    parts = rows.astype(F32).reshape(16, 2, 8, 128)
    return jnp.concatenate([parts[:, 0], parts[:, 1]], axis=-1).reshape(CELLS, E)


def attend(cells, w_q, w_k, w_v):
    queries = mm(cells, w_q)
    lookups = mm(cells, w_k).astype(BF)
    values = mm(cells, w_v)
    head = iota2((128, E), 1) >> 5
    query_set = jnp.concatenate(
        [jnp.where(head == h, queries, 0.0).astype(BF) for h in range(H)], axis=0
    )
    weights = softmax(mm(query_set, lookups, NT))
    mixed = jnp.zeros((128, E), F32)
    for h in range(H):
        mixed = mixed + mm(
            weights[128 * h : 128 * (h + 1)], jnp.where(head == h, values, 0.0).astype(BF)
        )
    return mixed


def main_kernel(
    surface, coupling, w_stencil, w_patch, w_query, w_key, w_value, w_out, w_unpatch,
    state, zt,
    surf, cp, wst, wp, wu, wq, wqkvo, sw, am, s_ref, bb,
    row_s, col_s, row_r, col_r, corner_r,
    g0, k0, v0, n1, g1, mix1, m1,
    load_sem, halo_send, halo_recv, gather_send, gather_recv, a2a_send, a2a_recv,
):
    row = lax.axis_index("row")
    col = lax.axis_index("col")
    row_bits = [lax.rem(lax.div(row, 1 << n), 2) for n in range(4)]
    col_bits = [lax.rem(lax.div(col, 1 << n), 2) for n in range(3)]

    row_r[...] = jnp.zeros_like(row_r)
    col_r[...] = jnp.zeros_like(col_r)
    corner_r[...] = jnp.zeros_like(corner_r)

    def has(step):
        dr, dc = step
        ok = row >= 0
        if dr < 0:
            ok = row > 0
        if dr > 0:
            ok = row < NR - 1
        if dc < 0:
            ok = ok & (col > 0)
        if dc > 0:
            ok = ok & (col < NC - 1)
        return ok

    barrier = pltpu.get_barrier_semaphore()
    for d in range(1, NC):
        pl.semaphore_signal(
            barrier, inc=1, device_id=(row, lax.rem(col + d, NC)), device_id_type=MESH
        )
    for d in range(1, NR):
        pl.semaphore_signal(
            barrier, inc=1, device_id=(lax.rem(row + d, NR), col), device_id_type=MESH
        )
    expected = jnp.int32(NC - 1 + NR - 1)
    for step in STEPS[4:]:
        @pl.when(has(step))
        def _():
            pl.semaphore_signal(
                barrier, inc=1, device_id=(row + step[0], col + step[1]), device_id_type=MESH
            )

        expected = expected + jnp.where(has(step), 1, 0)

    loads = []

    def load(src, dst):
        copy = pltpu.make_async_copy(src, dst, load_sem.at[len(loads)])
        copy.start()
        loads.append(copy)

    for i in range(8):
        load(surface.at[:, pl.ds(16 * i, 16), :], surf.at[:, pl.ds(16 * i, 16), :])
    for l in range(LAYERS):
        load(coupling.at[l], cp.at[l, pl.ds(8, TX), pl.ds(0, TY)])
    load(w_stencil, wst)
    load(w_patch, wp)
    for n, w in enumerate((w_query, w_key, w_value, w_out)):
        load(w, wqkvo.at[n])
    load(w_unpatch, wu)

    sw[...] = swap_matrix()

    for i in range(8):
        loads[i].wait()
        high = surf[:, 16 * i : 16 * (i + 1), :].reshape(256, TY).astype(BF)
        bb[0, pl.ds((8 + 16 * i) * C, 256), 0:TY] = mm(sw[...], high).astype(BF)

    strip = jnp.zeros((32, 512), F32)
    for k in range(4):
        strip = strip + mm(
            strip_select(k, TY, 0, TY - 3), bb[0, pl.ds((8 + 32 * k) * C, 512), 0:TY], NT
        )
    strip = strip.astype(BF)
    for l in range(2):
        loads[8 + l].wait()
    cols = jnp.zeros((32, TX), F32)
    rows_c = jnp.zeros((32, TY), F32)
    for l in range(2):
        field = cp[l, 8 : 8 + TX, 0:TY].astype(BF)
        cols = cols + mm(strip_select(l, TY, 0, TY - 3), field, NT)
        rows_c = rows_c + mm(strip_select(l, TX, 0, TX - 3), field)
    cols = cols.astype(BF)
    rows_c = rows_c.astype(BF)
    for side in range(2):
        half = slice(16 * side, 16 * (side + 1))
        col_s[side, :, 0:128] = cols[half]
        col_s[side, :, 128:640] = strip[half]
        col_s[side, :, 640:768] = cols[half]
        row_s[side, 48:64, :] = rows_c[half]
    row_s[0, 0:48, :] = bb[0, 8 * C : 11 * C, 0:TY]
    row_s[1, 0:48, :] = bb[0, (5 + TX) * C : (8 + TX) * C, 0:TY]

    pl.semaphore_wait(barrier, expected)

    lower = pl.ds(0, 256)
    upper = pl.ds(512, 256)
    pieces = (
        (row_s.at[0], row_r.at[1]),
        (row_s.at[1], row_r.at[0]),
        (col_s.at[0], col_r.at[1]),
        (col_s.at[1], col_r.at[0]),
        (col_s.at[0, :, lower], corner_r.at[3]),
        (col_s.at[1, :, lower], corner_r.at[2]),
        (col_s.at[0, :, upper], corner_r.at[1]),
        (col_s.at[1, :, upper], corner_r.at[0]),
    )

    def halo_copy(d):
        src, dst = pieces[d]
        return pltpu.make_async_remote_copy(
            src_ref=src,
            dst_ref=dst,
            send_sem=halo_send.at[d],
            recv_sem=halo_recv.at[OPPOSITE[d]],
            device_id=(row + STEPS[d][0], col + STEPS[d][1]),
            device_id_type=MESH,
        )

    for d in (4, 5, 6, 7, 2, 3, 0, 1):
        @pl.when(has(STEPS[d]))
        def _():
            halo_copy(d).start()

    for i in range(8):
        block = surf[:, 16 * i : 16 * (i + 1), :].reshape(256, TY)
        low = (block - block.astype(BF).astype(F32)).astype(BF)
        rows = pl.ds((8 + 16 * i) * C, 256)
        s_ref[rows, 0:TY] = bb[0, rows, 0:TY].astype(F32) + mm(sw[...], low)

    s_ref[0:80, 0:TY] = jnp.zeros((80, TY), F32)
    s_ref[139 * 16 : U * 16, 0:TY] = jnp.zeros((80, TY), F32)
    bb[0, 0:80, 0:TY] = jnp.zeros((80, TY), BF)
    bb[0, 139 * 16 : U * 16, 0:TY] = jnp.zeros((80, TY), BF)
    bb[1, 0:96, :] = jnp.zeros((96, W), BF)
    bb[1, 138 * 16 : U * 16, :] = jnp.zeros((96, W), BF)
    cp[2, 0:8, :] = jnp.zeros((8, W), F32)
    cp[2, 8 + TX : U, :] = jnp.zeros((8, W), F32)
    cp[2, 8 : 8 + TX, TY:W] = jnp.zeros((TX, 128), F32)

    loads[10].wait()
    loads[11].wait()
    spread = ones_where((iota2((C, DEPTH), 1) & 15) == iota2((C, DEPTH), 0))
    tiled = mm(wst[...].astype(BF), spread)
    band = iota2((C, DEPTH), 1) >> 4
    for l in range(LAYERS):
        for b in range(3):
            pick = [
                tiled[((l * 9 + a * 3 + b) * C) : ((l * 9 + a * 3 + b) * C) + C] for a in range(3)
            ]
            for xo in range(G):
                block = jnp.where(
                    band == xo,
                    pick[0],
                    jnp.where(
                        band == xo + 1, pick[1], jnp.where(band == xo + 2, pick[2], 0.0)
                    ),
                )
                am[l, C * xo : C * (xo + 1), DEPTH * b : DEPTH * (b + 1)] = block.astype(BF)

    loads[12].wait()
    for p in range(PATCH):
        turned = mm(sw[...], wp[:, p, :, :].reshape(256, E))
        wq[:, C * p : C * (p + 1), :] = turned.astype(BF).reshape(PATCH, C, E)
    for n in range(4):
        loads[13 + n].wait()

    for d in range(8):
        @pl.when(has(STEPS[d]))
        def _():
            halo_copy(OPPOSITE[d]).wait_recv()

    for side, u, first in ((0, 5, 5), (1, 8 + TX, 0)):
        halo = row_r[side, 0:48, :]
        s_ref[u * C : (u + 3) * C, 0:TY] = halo.astype(F32)
        bb[0, u * C : (u + 3) * C, 0:TY] = halo
        for l in range(2):
            at = iota2((8, 16), 0) - first
            s = iota2((8, 16), 1) - 4 * l
            pick = ones_where((at == s) & (s >= 0) & (s < 3))
            top = 0 if side == 0 else 8 + TX
            cp[l, top : top + 8, 0:TY] = mm(pick, row_r[side, 48:64, :])
    def place(rows, strip, k):
        columns = mm(strip, strip_place(k), TN)
        s_ref[rows, TY:W] = columns
        bb[0, rows, TY:W] = columns.astype(BF)

    both = jnp.concatenate([col_r[0, :, 128:640], col_r[1, :, 128:640]], axis=0)
    both_c = jnp.concatenate([col_r[0, :, 0:128], col_r[1, :, 0:128]], axis=0)
    for k in range(4):
        place(pl.ds((8 + 32 * k) * C, 512), both, k)
    for l in range(2):
        cp[l, 8 : 8 + TX, TY:W] = mm(both_c, strip_place(l), TN)
    above = jnp.concatenate([corner_r[0], corner_r[1]], axis=0)
    below = jnp.concatenate([corner_r[2], corner_r[3]], axis=0)
    place(pl.ds(0, 128), above[:, 0:128], 3)
    place(pl.ds((8 + TX) * C, 128), below[:, 128:256], 0)
    for l in range(2):
        cp[l, 0:8, TY:W] = mm(above[:, 128:256], strip_place(l), TN)[TX - 8 : TX]
        cp[l, 8 + TX : U, TY:W] = mm(below[:, 0:128], strip_place(l), TN)[0:8]

    def gather(half, d):
        cells = pl.ds(64 * half, 64)
        return pltpu.make_async_remote_copy(
            src_ref=g0.at[0, cells],
            dst_ref=g0.at[d, cells],
            send_sem=gather_send.at[half, d],
            recv_sem=gather_recv.at[half, d],
            device_id=(row, flipped(col_bits, d)),
            device_id_type=MESH,
        )

    def shifted(src, u):
        window = bb[src, (u - 1) * C : (u - 1) * C + DEPTH, :]
        return jnp.concatenate(
            [
                jnp.concatenate([window[:, W - 1 :], window[:, : W - 1]], axis=1),
                window,
                jnp.concatenate([window[:, 1:], window[:, :1]], axis=1),
            ],
            axis=0,
        )

    def update(l, u, gain, lanes):
        for x in range(G):
            if u + x > 137 - l:
                continue
            rows = slice((u + x) * C, (u + x + 1) * C)
            new = s_ref[rows, lanes] + cp[l, u + x : u + x + 1, lanes] * (
                gain[C * x : C * (x + 1)]
            )
            s_ref[rows, lanes] = new
            bb[(l + 1) % 2, rows, lanes] = new.astype(BF)

    def advance(l, pair):
        starts = [6 + l + G * (2 * pair + n) for n in range(2)]
        windows = [shifted(l % 2, u) for u in starts]
        for u, window in zip(starts, windows):
            update(l, u, jnp.tanh(mm(am[l], window[:, :TY])), slice(0, TY))
        if l < LAYERS - 1:
            edges = jnp.tanh(
                mm(am[l], jnp.concatenate([window[:, TY:] for window in windows], axis=1))
            )
            for n, u in enumerate(starts):
                update(l, u, edges[:, 128 * n : 128 * (n + 1)], slice(TY, W))

    last = LAYERS % 2

    def patch(half):
        for i in range(4 * half, 4 * half + 4):
            block = bb[last, pl.ds((8 + 16 * i) * C, 256), 0:TY]
            zt[i] = mm(sw[...], block, NT).astype(BF)
        part = jnp.zeros((CELLS // 2, E), F32)
        for q in range(PATCH):
            block = zt[4 * half : 4 * half + 4, 16 * q : 16 * (q + 1), :]
            part = part + mm(block.reshape(CELLS // 2, 256), wq[q])
        g0[0, 64 * half : 64 * half + 64, :] = normed(part)
        for d in COL_ORDER:
            gather(half, d).start()
        return part

    parts = []
    for step in range(11 + 2 * (LAYERS - 1)):
        for l in range(LAYERS):
            pair = step - 2 * l
            if 0 <= pair < 11:
                advance(l, pair)
                if l == LAYERS - 1 and pair == 5:
                    parts.append(patch(0))
    parts.append(patch(1))
    coarse = jnp.concatenate(parts, axis=0)

    def a2a(phase, src, dst, d):
        rows = pl.ds(16 * d, 16)
        return pltpu.make_async_remote_copy(
            src_ref=src.at[rows],
            dst_ref=dst.at[rows],
            send_sem=a2a_send.at[phase, d],
            recv_sem=a2a_recv.at[phase],
            device_id=(flipped(row_bits, d), col),
            device_id_type=MESH,
        )

    def exchange(phase, src, dst):
        for d in ROW_ORDER:
            a2a(phase, src, dst, d).start()
        dst[0:16, :] = src[0:16, :]
        rest = pl.ds(16, 16 * (NR - 1))
        pltpu.make_async_remote_copy(
            src_ref=src.at[rest],
            dst_ref=dst.at[rest],
            send_sem=a2a_send.at[phase, 1],
            recv_sem=a2a_recv.at[phase],
            device_id=(flipped(row_bits, 1), col),
            device_id_type=MESH,
        ).wait_recv()

    def state_back():
        for i in range(8):
            block = s_ref[pl.ds((8 + 16 * i) * C, 256), 0:TY]
            high = block.astype(BF)
            low = (block - high.astype(F32)).astype(BF)
            turned = mm(sw[...], high) + mm(sw[...], low)
            state[:, 16 * i : 16 * (i + 1), :] = turned.reshape(C, 16, TY)

    def unpatch_weights():
        loads[17].wait()
        for c in range(C):
            turned = mm(sw[...], wu[:, 256 * c : 256 * (c + 1)], NT).astype(BF)
            wq[:, C * c : C * (c + 1), :] = turned.reshape(PATCH, C, E)

    state_back()
    head = iota2((16, E), 1) >> 5
    queries = mm(g0[0], wqkvo[0, 0])
    unpatch_weights()
    mixed = []
    for half in range(2):
        cells = slice(64 * half, 64 * half + 64)
        for d in (0,) + GATHER_ORDER:
            if d > 0:
                gather(half, d).wait_recv()
            k0[d, cells, :] = mm(g0[d, cells, :], wqkvo[1, 0]).astype(BF)
            v0[d, cells, :] = mm(g0[d, cells, :], wqkvo[2, 0]).astype(BF)
        for i in range(4 * half, 4 * half + 4):
            rows = slice(16 * i, 16 * (i + 1))
            query_set = jnp.concatenate(
                [jnp.where(head == h, queries[rows], 0.0).astype(BF) for h in range(H)], axis=0
            )
            weights = softmax(mm(query_set, k0[:, rows, :].reshape(128, E), NT))
            whole = mm(weights, v0[:, rows, :].reshape(128, E))
            mixed.append(
                sum(jnp.where(head == h, whole[16 * h : 16 * (h + 1)], 0.0) for h in range(H))
            )
    coarse = coarse + mm(jnp.concatenate(mixed, axis=0).astype(BF), wqkvo[3, 0])

    r = iota2((CELLS, CELLS), 0)
    k = iota2((CELLS, CELLS), 1)
    turn = ones_where(k == (r & 7) * 16 + ((r >> 3) ^ row))
    n1[...] = packed(mm(turn, normed(coarse)))
    exchange(0, n1, g1)
    mix1[...] = packed(
        attend(unpacked(g1[...]).astype(BF), wqkvo[0, 1], wqkvo[1, 1], wqkvo[2, 1])
    )
    exchange(1, mix1, m1)
    back = mm(turn, unpacked(m1[...]).astype(BF), TN).astype(BF)
    coarse = coarse + mm(back, wqkvo[3, 1])
    coarse = coarse.astype(BF)
    for q in range(PATCH):
        cells = mm(coarse, wq[q], NT).astype(BF)
        zt[:, 16 * q : 16 * (q + 1), :] = cells.reshape(8, 16, 256)
    for d in range(8):
        @pl.when(has(STEPS[d]))
        def _():
            halo_copy(d).wait_send()

    for half in range(2):
        for d in COL_ORDER:
            gather(half, d).wait_send()
    for d in ROW_ORDER:
        a2a(0, n1, g1, d).wait_send()
        a2a(1, mix1, m1, d).wait_send()


def add_kernel(zt, state, out, swap, held, store_sem):
    swap[...] = swap_matrix()
    stores = []
    for i in range(8):
        rows = slice(16 * i, 16 * (i + 1))
        detail = mm(zt[i], swap[...], TN)
        held[:, rows, :] = state[:, rows, :] + detail.reshape(C, 16, TY)
        copy = pltpu.make_async_copy(held.at[:, rows, :], out.at[:, rows, :], store_sem.at[i])
        copy.start()
        stores.append(copy)
    for copy in stores:
        copy.wait()


def on_device(surface, coupling, w_stencil, w_patch, w_query, w_key, w_value, w_out, w_unpatch):
    anywhere = pl.BlockSpec(memory_space=pl.ANY)
    in_vmem = pl.BlockSpec(memory_space=pltpu.VMEM)
    state, cells = pl.pallas_call(
        main_kernel,
        out_shape=(pltpu.VMEM((C, TX, TY), F32), pltpu.VMEM((8, 256, 256), BF)),
        in_specs=[anywhere] * 9,
        out_specs=(in_vmem, in_vmem),
        scratch_shapes=[
            pltpu.VMEM((C, TX, TY), F32),
            pltpu.VMEM((LAYERS, U, W), F32),
            pltpu.VMEM((LAYERS * 9 * C, C), F32),
            pltpu.VMEM((C, PATCH, PATCH, E), BF),
            pltpu.VMEM((E, C * 256), BF),
            pltpu.VMEM((PATCH, 256, E), BF),
            pltpu.VMEM((4, 2, E, E), BF),
            pltpu.VMEM((256, 256), BF),
            pltpu.VMEM((LAYERS, G * C, 3 * DEPTH), BF),
            pltpu.VMEM((U * C, W), F32),
            pltpu.VMEM((2, U * C, W), BF),
            pltpu.VMEM((2, 64, TY), BF),
            pltpu.VMEM((2, 16, 768), BF),
            pltpu.VMEM((2, 64, TY), BF),
            pltpu.VMEM((2, 16, 768), BF),
            pltpu.VMEM((4, 16, 256), BF),
            pltpu.VMEM((NC, CELLS, E), BF),
            pltpu.VMEM((NC, CELLS, E), BF),
            pltpu.VMEM((NC, CELLS, E), BF),
            pltpu.VMEM((256, 128), BF),
            pltpu.VMEM((256, 128), BF),
            pltpu.VMEM((256, 128), BF),
            pltpu.VMEM((256, 128), BF),
            pltpu.SemaphoreType.DMA((18,)),
            pltpu.SemaphoreType.DMA((8,)),
            pltpu.SemaphoreType.DMA((8,)),
            pltpu.SemaphoreType.DMA((2, NC)),
            pltpu.SemaphoreType.DMA((2, NC)),
            pltpu.SemaphoreType.DMA((2, NR)),
            pltpu.SemaphoreType.DMA((2,)),
        ],
        compiler_params=pltpu.CompilerParams(
            collective_id=0, has_side_effects=True, vmem_limit_bytes=60 * 1024 * 1024
        ),
    )(
        surface,
        coupling,
        w_stencil.reshape(LAYERS * 9 * C, C),
        w_patch.reshape(C, PATCH, PATCH, E),
        w_query,
        w_key,
        w_value,
        w_out,
        w_unpatch,
    )
    return pl.pallas_call(
        add_kernel,
        out_shape=jax.ShapeDtypeStruct((C, TX, TY), F32),
        in_specs=[in_vmem, in_vmem],
        out_specs=anywhere,
        scratch_shapes=[
            pltpu.VMEM((256, 256), BF),
            pltpu.VMEM((C, TX, TY), F32),
            pltpu.SemaphoreType.DMA((8,)),
        ],
        compiler_params=pltpu.CompilerParams(vmem_limit_bytes=32 * 1024 * 1024),
    )(cells, state)


def solution(mesh):
    in_specs = (P(None, "row", "col"), P(None, "row", "col"), P(), P(), P(), P(), P(), P(), P())
    out_specs = P(None, "row", "col")
    return jax.shard_map(
        on_device, mesh=mesh, in_specs=in_specs, out_specs=out_specs, check_vma=False
    )
```

```python
import jax
import jax.numpy as jnp
from jax import lax
from jax.experimental import pallas as pl
from jax.experimental.pallas import tpu as pltpu
from jax.sharding import PartitionSpec as P

C = 16
E = 256
H = 8
PATCH = 16
LAYERS = 3
NR = 16
NC = 8
TX = 128
TY = 256
CELLS = 128
U = TX + 16
W = TY + 128
G = 6
DEPTH = (G + 2) * C
BF = jnp.bfloat16
F32 = jnp.float32
MESH = pl.DeviceIdType.MESH
NT = (((1,), (1,)), ((), ()))
TN = (((0,), (0,)), ((), ()))

STEPS = ((-1, 0), (1, 0), (0, -1), (0, 1), (-1, -1), (-1, 1), (1, -1), (1, 1))
OPPOSITE = (1, 0, 3, 2, 7, 6, 5, 4)
ROW_ORDER = (10, 11, 8, 9, 14, 15, 12, 13, 6, 7, 4, 5, 2, 3, 1)
COL_ORDER = (6, 5, 7, 2, 4, 1, 3)
GATHER_ORDER = (2, 1, 3, 4, 6, 5, 7)


def iota2(shape, dim):
    return lax.broadcasted_iota(jnp.int32, shape, dim)


def ones_where(mask):
    return jnp.where(mask, 1.0, 0.0).astype(BF)


def swap_matrix():
    row = iota2((256, 256), 0)
    col = iota2((256, 256), 1)
    return ones_where(col == (row & 15) * 16 + (row >> 4))


def mm(a, b, dims=None):
    if dims is None:
        return jnp.dot(a, b, preferred_element_type=F32)
    return lax.dot_general(a, b, dims, preferred_element_type=F32)


def strip_select(k, size, near, far):
    row = iota2((32, size), 0)
    at = iota2((32, size), 1)
    s = (row & 15) - 4 * k
    goal = jnp.where(row < 16, near, far) + s
    return ones_where((s >= 0) & (s < 3) & (at == goal))


def strip_place(k):
    return strip_select(k, 128, 125, 0)


def normed(coarse):
    mean = jnp.mean(coarse * coarse, axis=-1, keepdims=True)
    return (coarse * lax.rsqrt(mean + 1e-06)).astype(BF)


def powers_of(scores):
    scores = scores * (E // H) ** (-0.5)
    return jnp.exp(scores - jnp.max(scores, axis=-1, keepdims=True)).astype(BF)


def flipped(bits, d):
    return sum(((1 - bit) if (d >> n) & 1 else bit) * (1 << n) for n, bit in enumerate(bits))


def packed(cells):
    parts = cells.reshape(16, 8, E)
    return (
        jnp.stack([parts[:, :, :128], parts[:, :, 128:]], axis=1).reshape(256, 128).astype(BF)
    )


def unpacked(rows):
    parts = rows.astype(F32).reshape(16, 2, 8, 128)
    return jnp.concatenate([parts[:, 0], parts[:, 1]], axis=-1).reshape(CELLS, E)


def own_lanes(head, stacked):
    return sum(jnp.where(head == h, stacked[16 * h : 16 * (h + 1)], 0.0) for h in range(H))


def attend(cells, w_q, w_k_turned, w_v):
    queries = mm(cells, w_q).astype(BF)
    lookups = mm(w_k_turned, cells, NT)
    values = mm(cells, w_v)
    head = iota2((128, E), 1) >> 5
    channel_head = iota2((E, 128), 0) >> 5
    lookup_set = jnp.concatenate(
        [jnp.where(channel_head == h, lookups, 0.0).astype(BF) for h in range(H)], axis=1
    )
    scores = mm(queries, lookup_set)
    powers = jnp.concatenate(
        [powers_of(scores[:, 128 * h : 128 * (h + 1)]) for h in range(H)], axis=1
    )
    value_set = jnp.concatenate(
        [jnp.where(head == h, values, 0.0).astype(BF) for h in range(H)], axis=0
    )
    own_head = jnp.concatenate([ones_where(head == h) for h in range(H)], axis=0)
    return mm(powers, value_set) / mm(powers, own_head)


def main_kernel(
    surface, coupling, w_stencil, w_patch, w_query, w_key, w_value, w_out, w_unpatch,
    state, zt,
    surf, cp, wst, wp, wu, wq, wqkvo, wkt, sw, am, s_ref, bb,
    row_s, col_s, row_r, col_r, corner_r,
    g0, k0, v0, n1, g1, mix1, m1,
    load_sem, halo_send, halo_recv, gather_send, gather_recv, a2a_send, a2a_recv,
):
    row = lax.axis_index("row")
    col = lax.axis_index("col")
    row_bits = [lax.rem(lax.div(row, 1 << n), 2) for n in range(4)]
    col_bits = [lax.rem(lax.div(col, 1 << n), 2) for n in range(3)]

    row_r[...] = jnp.zeros_like(row_r)
    col_r[...] = jnp.zeros_like(col_r)
    corner_r[...] = jnp.zeros_like(corner_r)

    def has(step):
        dr, dc = step
        ok = row >= 0
        if dr < 0:
            ok = row > 0
        if dr > 0:
            ok = row < NR - 1
        if dc < 0:
            ok = ok & (col > 0)
        if dc > 0:
            ok = ok & (col < NC - 1)
        return ok

    barrier = pltpu.get_barrier_semaphore()
    expected = jnp.int32(0)
    for step in STEPS[4:] + STEPS[:4]:
        @pl.when(has(step))
        def _():
            pl.semaphore_signal(
                barrier, inc=1, device_id=(row + step[0], col + step[1]), device_id_type=MESH
            )

        expected = expected + jnp.where(has(step), 1, 0)
    loads = []

    def load(src, dst):
        copy = pltpu.make_async_copy(src, dst, load_sem.at[len(loads)])
        copy.start()
        loads.append(copy)

    for i in range(8):
        load(surface.at[:, pl.ds(16 * i, 16), :], surf.at[:, pl.ds(16 * i, 16), :])
    for l in range(LAYERS):
        load(coupling.at[l], cp.at[l, pl.ds(8, TX), pl.ds(0, TY)])
    load(w_stencil, wst)

    for d in COL_ORDER:
        pl.semaphore_signal(
            barrier, inc=1, device_id=(row, flipped(col_bits, d)), device_id_type=MESH
        )
    for d in ROW_ORDER:
        pl.semaphore_signal(
            barrier, inc=1, device_id=(flipped(row_bits, d), col), device_id_type=MESH
        )
    expected = expected + (NC - 1 + NR - 1)

    sw[...] = swap_matrix()

    for i in range(8):
        loads[i].wait()
        high = surf[:, 16 * i : 16 * (i + 1), :].reshape(256, TY).astype(BF)
        bb[0, pl.ds((8 + 16 * i) * C, 256), 0:TY] = mm(sw[...], high).astype(BF)

    load(w_patch, wp)
    for n, w in enumerate((w_query, w_key, w_value, w_out)):
        load(w, wqkvo.at[n])
    load(w_unpatch, wu)

    strip = jnp.zeros((32, 512), F32)
    for k in range(4):
        strip = strip + mm(
            strip_select(k, TY, 0, TY - 3), bb[0, pl.ds((8 + 32 * k) * C, 512), 0:TY], NT
        )
    strip = strip.astype(BF)
    for l in range(2):
        loads[8 + l].wait()
    cols = jnp.zeros((32, TX), F32)
    rows_c = jnp.zeros((32, TY), F32)
    for l in range(2):
        field = cp[l, 8 : 8 + TX, 0:TY].astype(BF)
        cols = cols + mm(strip_select(l, TY, 0, TY - 3), field, NT)
        rows_c = rows_c + mm(strip_select(l, TX, 0, TX - 3), field)
    cols = cols.astype(BF)
    rows_c = rows_c.astype(BF)
    for side in range(2):
        half = slice(16 * side, 16 * (side + 1))
        col_s[side, :, 0:128] = cols[half]
        col_s[side, :, 128:640] = strip[half]
        col_s[side, :, 640:768] = cols[half]
        row_s[side, 48:64, :] = rows_c[half]
    row_s[0, 0:48, :] = bb[0, 8 * C : 11 * C, 0:TY]
    row_s[1, 0:48, :] = bb[0, (5 + TX) * C : (8 + TX) * C, 0:TY]

    pl.semaphore_wait(barrier, expected)

    lower = pl.ds(0, 256)
    upper = pl.ds(512, 256)
    pieces = (
        (row_s.at[0], row_r.at[1]),
        (row_s.at[1], row_r.at[0]),
        (col_s.at[0], col_r.at[1]),
        (col_s.at[1], col_r.at[0]),
        (col_s.at[0, :, lower], corner_r.at[3]),
        (col_s.at[1, :, lower], corner_r.at[2]),
        (col_s.at[0, :, upper], corner_r.at[1]),
        (col_s.at[1, :, upper], corner_r.at[0]),
    )

    def halo_copy(d):
        src, dst = pieces[d]
        return pltpu.make_async_remote_copy(
            src_ref=src,
            dst_ref=dst,
            send_sem=halo_send.at[d],
            recv_sem=halo_recv.at[OPPOSITE[d]],
            device_id=(row + STEPS[d][0], col + STEPS[d][1]),
            device_id_type=MESH,
        )

    for d in (4, 5, 6, 7, 2, 3, 0, 1):
        @pl.when(has(STEPS[d]))
        def _():
            halo_copy(d).start()

    for i in range(8):
        block = surf[:, 16 * i : 16 * (i + 1), :].reshape(256, TY)
        low = (block - block.astype(BF).astype(F32)).astype(BF)
        rows = pl.ds((8 + 16 * i) * C, 256)
        s_ref[rows, 0:TY] = bb[0, rows, 0:TY].astype(F32) + mm(sw[...], low)

    s_ref[0:80, 0:TY] = jnp.zeros((80, TY), F32)
    s_ref[139 * 16 : U * 16, 0:TY] = jnp.zeros((80, TY), F32)
    bb[0, 0:80, 0:TY] = jnp.zeros((80, TY), BF)
    bb[0, 139 * 16 : U * 16, 0:TY] = jnp.zeros((80, TY), BF)
    bb[1, 0:96, :] = jnp.zeros((96, W), BF)
    bb[1, 138 * 16 : U * 16, :] = jnp.zeros((96, W), BF)
    cp[2, 0:8, :] = jnp.zeros((8, W), F32)
    cp[2, 8 + TX : U, :] = jnp.zeros((8, W), F32)
    cp[2, 8 : 8 + TX, TY:W] = jnp.zeros((TX, 128), F32)

    loads[10].wait()
    loads[11].wait()
    spread = ones_where((iota2((C, DEPTH), 1) & 15) == iota2((C, DEPTH), 0))
    tiled = mm(wst[...].astype(BF), spread)
    band = iota2((C, DEPTH), 1) >> 4
    for l in range(LAYERS):
        for b in range(3):
            pick = [
                tiled[((l * 9 + a * 3 + b) * C) : ((l * 9 + a * 3 + b) * C) + C] for a in range(3)
            ]
            for xo in range(G):
                block = jnp.where(
                    band == xo,
                    pick[0],
                    jnp.where(
                        band == xo + 1, pick[1], jnp.where(band == xo + 2, pick[2], 0.0)
                    ),
                )
                am[l, C * xo : C * (xo + 1), DEPTH * b : DEPTH * (b + 1)] = block.astype(BF)

    loads[12].wait()
    for p in range(PATCH):
        turned = mm(sw[...], wp[:, p, :, :].reshape(256, E))
        wq[:, C * p : C * (p + 1), :] = turned.astype(BF).reshape(PATCH, C, E)
    for n in range(4):
        loads[13 + n].wait()

    for d in range(8):
        @pl.when(has(STEPS[d]))
        def _():
            halo_copy(OPPOSITE[d]).wait_recv()

    for side, u, first in ((0, 5, 5), (1, 8 + TX, 0)):
        halo = row_r[side, 0:48, :]
        s_ref[u * C : (u + 3) * C, 0:TY] = halo.astype(F32)
        bb[0, u * C : (u + 3) * C, 0:TY] = halo
        for l in range(2):
            at = iota2((8, 16), 0) - first
            s = iota2((8, 16), 1) - 4 * l
            pick = ones_where((at == s) & (s >= 0) & (s < 3))
            top = 0 if side == 0 else 8 + TX
            cp[l, top : top + 8, 0:TY] = mm(pick, row_r[side, 48:64, :])
    def place(rows, strip, k):
        columns = mm(strip, strip_place(k), TN)
        s_ref[rows, TY:W] = columns
        bb[0, rows, TY:W] = columns.astype(BF)

    both = jnp.concatenate([col_r[0, :, 128:640], col_r[1, :, 128:640]], axis=0)
    both_c = jnp.concatenate([col_r[0, :, 0:128], col_r[1, :, 0:128]], axis=0)
    for k in range(4):
        place(pl.ds((8 + 32 * k) * C, 512), both, k)
    for l in range(2):
        cp[l, 8 : 8 + TX, TY:W] = mm(both_c, strip_place(l), TN)
    above = jnp.concatenate([corner_r[0], corner_r[1]], axis=0)
    below = jnp.concatenate([corner_r[2], corner_r[3]], axis=0)
    place(pl.ds(0, 128), above[:, 0:128], 3)
    place(pl.ds((8 + TX) * C, 128), below[:, 128:256], 0)
    for l in range(2):
        cp[l, 0:8, TY:W] = mm(above[:, 128:256], strip_place(l), TN)[TX - 8 : TX]
        cp[l, 8 + TX : U, TY:W] = mm(below[:, 0:128], strip_place(l), TN)[0:8]

    def gather(half, d, peer=None):
        cells = pl.ds(64 * half, 64)
        return pltpu.make_async_remote_copy(
            src_ref=g0.at[0, cells],
            dst_ref=g0.at[d, cells],
            send_sem=gather_send.at[half, d],
            recv_sem=gather_recv.at[half, d],
            device_id=(row, flipped(col_bits, d) if peer is None else peer),
            device_id_type=MESH,
        )

    def shifted(src, u):
        window = bb[src, (u - 1) * C : (u - 1) * C + DEPTH, :]
        return jnp.concatenate(
            [
                jnp.concatenate([window[:, W - 1 :], window[:, : W - 1]], axis=1),
                window,
                jnp.concatenate([window[:, 1:], window[:, :1]], axis=1),
            ],
            axis=0,
        )

    def update(l, u, gain, lanes):
        for x in range(G):
            if u + x > 137 - l:
                continue
            rows = slice((u + x) * C, (u + x + 1) * C)
            new = s_ref[rows, lanes] + cp[l, u + x : u + x + 1, lanes] * (
                gain[C * x : C * (x + 1)]
            )
            s_ref[rows, lanes] = new
            bb[(l + 1) % 2, rows, lanes] = new.astype(BF)

    def advance(l, pair):
        starts = [6 + l + G * (2 * pair + n) for n in range(2)]
        windows = [shifted(l % 2, u) for u in starts]
        for u, window in zip(starts, windows):
            update(l, u, jnp.tanh(mm(am[l], window[:, :TY])), slice(0, TY))
        if l < LAYERS - 1:
            edges = jnp.tanh(
                mm(am[l], jnp.concatenate([window[:, TY:] for window in windows], axis=1))
            )
            for n, u in enumerate(starts):
                update(l, u, edges[:, 128 * n : 128 * (n + 1)], slice(TY, W))

    last = LAYERS % 2

    def patch(half):
        for i in range(4 * half, 4 * half + 4):
            block = bb[last, pl.ds((8 + 16 * i) * C, 256), 0:TY]
            zt[i] = mm(sw[...], block, NT).astype(BF)
        part = jnp.zeros((CELLS // 2, E), F32)
        for q in range(PATCH):
            block = zt[4 * half : 4 * half + 4, 16 * q : 16 * (q + 1), :]
            part = part + mm(block.reshape(CELLS // 2, 256), wq[q])
        g0[0, 64 * half : 64 * half + 64, :] = normed(part)
        for target in range(NC):
            @pl.when(col != target)
            def _():
                gather(half, flipped(col_bits, target), target).start()

        return part

    parts = []
    for step in range(11 + 2 * (LAYERS - 1)):
        for l in range(LAYERS):
            pair = step - 2 * l
            if 0 <= pair < 11:
                advance(l, pair)
                if l == LAYERS - 1 and pair == 5:
                    parts.append(patch(0))
    parts.append(patch(1))
    coarse = jnp.concatenate(parts, axis=0)

    def a2a(phase, src, dst, d):
        rows = pl.ds(16 * d, 16)
        return pltpu.make_async_remote_copy(
            src_ref=src.at[rows],
            dst_ref=dst.at[rows],
            send_sem=a2a_send.at[phase, d],
            recv_sem=a2a_recv.at[phase],
            device_id=(flipped(row_bits, d), col),
            device_id_type=MESH,
        )

    def exchange(phase, src, dst):
        for d in ROW_ORDER:
            a2a(phase, src, dst, d).start()
        dst[0:16, :] = src[0:16, :]
        rest = pl.ds(16, 16 * (NR - 1))
        pltpu.make_async_remote_copy(
            src_ref=src.at[rest],
            dst_ref=dst.at[rest],
            send_sem=a2a_send.at[phase, 1],
            recv_sem=a2a_recv.at[phase],
            device_id=(flipped(row_bits, 1), col),
            device_id_type=MESH,
        ).wait_recv()

    def state_back():
        for i in range(8):
            block = s_ref[pl.ds((8 + 16 * i) * C, 256), 0:TY]
            high = block.astype(BF)
            low = (block - high.astype(F32)).astype(BF)
            turned = mm(sw[...], high) + mm(sw[...], low)
            state[:, 16 * i : 16 * (i + 1), :] = turned.reshape(C, 16, TY)

    def unpatch_weights():
        one = ones_where(iota2((E, E), 0) == iota2((E, E), 1))
        wkt[...] = mm(wqkvo[1, 1], one, TN).astype(BF)
        loads[17].wait()
        for c in range(C):
            turned = mm(sw[...], wu[:, 256 * c : 256 * (c + 1)], NT).astype(BF)
            wq[:, C * c : C * (c + 1), :] = turned.reshape(PATCH, C, E)

    state_back()
    head = iota2((16, E), 1) >> 5
    queries = mm(g0[0], wqkvo[0, 0])
    unpatch_weights()
    mixed = []
    for half in range(2):
        cells = slice(64 * half, 64 * half + 64)
        for d in (0,) + GATHER_ORDER:
            if d > 0:
                gather(half, d).wait_recv()
            k0[d, cells, :] = mm(g0[d, cells, :], wqkvo[1, 0]).astype(BF)
            v0[d, cells, :] = mm(g0[d, cells, :], wqkvo[2, 0]).astype(BF)
        for i in range(4 * half, 4 * half + 4):
            rows = slice(16 * i, 16 * (i + 1))
            query_set = jnp.concatenate(
                [jnp.where(head == h, queries[rows], 0.0).astype(BF) for h in range(H)], axis=0
            )
            powers = powers_of(mm(query_set, k0[:, rows, :].reshape(128, E), NT))
            whole = mm(powers, v0[:, rows, :].reshape(128, E))
            total = mm(powers, jnp.ones((128, E), BF))
            mixed.append(own_lanes(head, whole) / own_lanes(head, total))
    coarse = coarse + mm(jnp.concatenate(mixed, axis=0).astype(BF), wqkvo[3, 0])

    r = iota2((CELLS, CELLS), 0)
    k = iota2((CELLS, CELLS), 1)
    turn = ones_where(k == (r & 7) * 16 + ((r >> 3) ^ row))
    n1[...] = packed(mm(turn, normed(coarse)))
    exchange(0, n1, g1)
    mix1[...] = packed(
        attend(unpacked(g1[...]).astype(BF), wqkvo[0, 1], wkt[...], wqkvo[2, 1])
    )
    exchange(1, mix1, m1)
    back = mm(turn, unpacked(m1[...]).astype(BF), TN).astype(BF)
    coarse = coarse + mm(back, wqkvo[3, 1])
    coarse = coarse.astype(BF)
    for q in range(PATCH):
        cells = mm(coarse, wq[q], NT).astype(BF)
        zt[:, 16 * q : 16 * (q + 1), :] = cells.reshape(8, 16, 256)
    for d in range(8):
        @pl.when(has(STEPS[d]))
        def _():
            halo_copy(d).wait_send()

    for half in range(2):
        for d in COL_ORDER:
            gather(half, d).wait_send()
    for d in ROW_ORDER:
        a2a(0, n1, g1, d).wait_send()
        a2a(1, mix1, m1, d).wait_send()


def add_kernel(zt, state, out, swap, held, store_sem):
    swap[...] = swap_matrix()
    stores = []
    for i in range(8):
        rows = slice(16 * i, 16 * (i + 1))
        detail = mm(zt[i], swap[...], TN)
        held[:, rows, :] = state[:, rows, :] + detail.reshape(C, 16, TY)
        copy = pltpu.make_async_copy(held.at[:, rows, :], out.at[:, rows, :], store_sem.at[i])
        copy.start()
        stores.append(copy)
    for copy in stores:
        copy.wait()


def on_device(surface, coupling, w_stencil, w_patch, w_query, w_key, w_value, w_out, w_unpatch):
    anywhere = pl.BlockSpec(memory_space=pl.ANY)
    in_vmem = pl.BlockSpec(memory_space=pltpu.VMEM)
    state, cells = pl.pallas_call(
        main_kernel,
        out_shape=(pltpu.VMEM((C, TX, TY), F32), pltpu.VMEM((8, 256, 256), BF)),
        in_specs=[anywhere] * 9,
        out_specs=(in_vmem, in_vmem),
        scratch_shapes=[
            pltpu.VMEM((C, TX, TY), F32),
            pltpu.VMEM((LAYERS, U, W), F32),
            pltpu.VMEM((LAYERS * 9 * C, C), F32),
            pltpu.VMEM((C, PATCH, PATCH, E), BF),
            pltpu.VMEM((E, C * 256), BF),
            pltpu.VMEM((PATCH, 256, E), BF),
            pltpu.VMEM((4, 2, E, E), BF),
            pltpu.VMEM((E, E), BF),
            pltpu.VMEM((256, 256), BF),
            pltpu.VMEM((LAYERS, G * C, 3 * DEPTH), BF),
            pltpu.VMEM((U * C, W), F32),
            pltpu.VMEM((2, U * C, W), BF),
            pltpu.VMEM((2, 64, TY), BF),
            pltpu.VMEM((2, 16, 768), BF),
            pltpu.VMEM((2, 64, TY), BF),
            pltpu.VMEM((2, 16, 768), BF),
            pltpu.VMEM((4, 16, 256), BF),
            pltpu.VMEM((NC, CELLS, E), BF),
            pltpu.VMEM((NC, CELLS, E), BF),
            pltpu.VMEM((NC, CELLS, E), BF),
            pltpu.VMEM((256, 128), BF),
            pltpu.VMEM((256, 128), BF),
            pltpu.VMEM((256, 128), BF),
            pltpu.VMEM((256, 128), BF),
            pltpu.SemaphoreType.DMA((18,)),
            pltpu.SemaphoreType.DMA((8,)),
            pltpu.SemaphoreType.DMA((8,)),
            pltpu.SemaphoreType.DMA((2, NC)),
            pltpu.SemaphoreType.DMA((2, NC)),
            pltpu.SemaphoreType.DMA((2, NR)),
            pltpu.SemaphoreType.DMA((2,)),
        ],
        compiler_params=pltpu.CompilerParams(
            collective_id=0, has_side_effects=True, vmem_limit_bytes=60 * 1024 * 1024
        ),
    )(
        surface,
        coupling,
        w_stencil.reshape(LAYERS * 9 * C, C),
        w_patch.reshape(C, PATCH, PATCH, E),
        w_query,
        w_key,
        w_value,
        w_out,
        w_unpatch,
    )
    return pl.pallas_call(
        add_kernel,
        out_shape=jax.ShapeDtypeStruct((C, TX, TY), F32),
        in_specs=[in_vmem, in_vmem],
        out_specs=anywhere,
        scratch_shapes=[
            pltpu.VMEM((256, 256), BF),
            pltpu.VMEM((C, TX, TY), F32),
            pltpu.SemaphoreType.DMA((8,)),
        ],
        compiler_params=pltpu.CompilerParams(vmem_limit_bytes=32 * 1024 * 1024),
    )(cells, state)


def solution(mesh):
    in_specs = (P(None, "row", "col"), P(None, "row", "col"), P(), P(), P(), P(), P(), P(), P())
    out_specs = P(None, "row", "col")
    return jax.shard_map(
        on_device, mesh=mesh, in_specs=in_specs, out_specs=out_specs, check_vma=False
    )
```

```python
import jax
import jax.numpy as jnp
from jax import lax
from jax.experimental import pallas as pl
from jax.experimental.pallas import tpu as pltpu
from jax.sharding import PartitionSpec as P

C = 16
E = 256
H = 8
PATCH = 16
LAYERS = 3
NR = 16
NC = 8
TX = 128
TY = 256
CELLS = 128
U = TX + 16
W = TY + 128
G = 6
DEPTH = (G + 2) * C
BF = jnp.bfloat16
F32 = jnp.float32
MESH = pl.DeviceIdType.MESH
NT = (((1,), (1,)), ((), ()))
TN = (((0,), (0,)), ((), ()))

STEPS = ((-1, 0), (1, 0), (0, -1), (0, 1), (-1, -1), (-1, 1), (1, -1), (1, 1))
OPPOSITE = (1, 0, 3, 2, 7, 6, 5, 4)
ROW_ORDER = (10, 11, 8, 9, 14, 15, 12, 13, 6, 7, 4, 5, 2, 3, 1)
COL_ORDER = (6, 5, 7, 2, 4, 1, 3)
GATHER_ORDER = (2, 1, 3, 4, 6, 5, 7)
PARTS = ((0, 3), (3, 8))


def iota2(shape, dim):
    return lax.broadcasted_iota(jnp.int32, shape, dim)


def ones_where(mask):
    return jnp.where(mask, 1.0, 0.0).astype(BF)


def swap_matrix():
    row = iota2((256, 256), 0)
    col = iota2((256, 256), 1)
    return ones_where(col == (row & 15) * 16 + (row >> 4))


def mm(a, b, dims=None):
    if dims is None:
        return jnp.dot(a, b, preferred_element_type=F32)
    return lax.dot_general(a, b, dims, preferred_element_type=F32)


def strip_select(k, size, near, far):
    row = iota2((32, size), 0)
    at = iota2((32, size), 1)
    s = (row & 15) - 4 * k
    goal = jnp.where(row < 16, near, far) + s
    return ones_where((s >= 0) & (s < 3) & (at == goal))


def strip_place(k):
    return strip_select(k, 128, 125, 0)


def normed(coarse):
    mean = jnp.mean(coarse * coarse, axis=-1, keepdims=True)
    return (coarse * lax.rsqrt(mean + 1e-06)).astype(BF)


def powers_of(scores):
    scores = scores * (E // H) ** (-0.5)
    return jnp.exp(scores - jnp.max(scores, axis=-1, keepdims=True)).astype(BF)


def flipped(bits, d):
    return sum(((1 - bit) if (d >> n) & 1 else bit) * (1 << n) for n, bit in enumerate(bits))


def packed(cells):
    parts = cells.reshape(16, 8, E)
    return (
        jnp.stack([parts[:, :, :128], parts[:, :, 128:]], axis=1).reshape(256, 128).astype(BF)
    )


def unpacked(rows):
    parts = rows.astype(F32).reshape(16, 2, 8, 128)
    return jnp.concatenate([parts[:, 0], parts[:, 1]], axis=-1).reshape(CELLS, E)


def own_lanes(head, stacked):
    return sum(jnp.where(head == h, stacked[16 * h : 16 * (h + 1)], 0.0) for h in range(H))


def attend(cells, w_q, w_k_turned, w_v):
    queries = mm(cells, w_q).astype(BF)
    lookups = mm(w_k_turned, cells, NT)
    values = mm(cells, w_v)
    head = iota2((128, E), 1) >> 5
    channel_head = iota2((E, 128), 0) >> 5
    lookup_set = jnp.concatenate(
        [jnp.where(channel_head == h, lookups, 0.0).astype(BF) for h in range(H)], axis=1
    )
    scores = mm(queries, lookup_set)
    powers = jnp.concatenate(
        [powers_of(scores[:, 128 * h : 128 * (h + 1)]) for h in range(H)], axis=1
    )
    value_set = jnp.concatenate(
        [jnp.where(head == h, values, 0.0).astype(BF) for h in range(H)], axis=0
    )
    own_head = jnp.concatenate([ones_where(head == h) for h in range(H)], axis=0)
    return mm(powers, value_set) / mm(powers, own_head)


def main_kernel(
    surface, coupling, w_stencil, w_patch, w_query, w_key, w_value, w_out, w_unpatch,
    state, zt,
    surf, cp, wst, wp, wu, wq, wqkvo, wkt, sw, am, s_ref, bb,
    row_s, col_s, row_r, col_r, corner_r,
    g0, k0, v0, n1, g1, mix1, m1,
    load_sem, halo_send, halo_recv, gather_send, gather_recv, a2a_send, a2a_recv,
):
    row = lax.axis_index("row")
    col = lax.axis_index("col")
    row_bits = [lax.rem(lax.div(row, 1 << n), 2) for n in range(4)]
    col_bits = [lax.rem(lax.div(col, 1 << n), 2) for n in range(3)]

    row_r[...] = jnp.zeros_like(row_r)
    col_r[...] = jnp.zeros_like(col_r)
    corner_r[...] = jnp.zeros_like(corner_r)

    def has(step):
        dr, dc = step
        ok = row >= 0
        if dr < 0:
            ok = row > 0
        if dr > 0:
            ok = row < NR - 1
        if dc < 0:
            ok = ok & (col > 0)
        if dc > 0:
            ok = ok & (col < NC - 1)
        return ok

    barrier = pltpu.get_barrier_semaphore()
    expected = jnp.int32(0)
    for step in STEPS[4:] + STEPS[:4]:
        @pl.when(has(step))
        def _():
            pl.semaphore_signal(
                barrier, inc=1, device_id=(row + step[0], col + step[1]), device_id_type=MESH
            )

        expected = expected + jnp.where(has(step), 1, 0)
    loads = []

    def load(src, dst):
        copy = pltpu.make_async_copy(src, dst, load_sem.at[len(loads)])
        copy.start()
        loads.append(copy)

    for i in range(8):
        load(surface.at[:, pl.ds(16 * i, 16), :], surf.at[:, pl.ds(16 * i, 16), :])
    for l in range(LAYERS):
        load(coupling.at[l], cp.at[l, pl.ds(8, TX), pl.ds(0, TY)])
    load(w_stencil, wst)

    for d in COL_ORDER:
        pl.semaphore_signal(
            barrier, inc=1, device_id=(row, flipped(col_bits, d)), device_id_type=MESH
        )
    for d in ROW_ORDER:
        pl.semaphore_signal(
            barrier, inc=1, device_id=(flipped(row_bits, d), col), device_id_type=MESH
        )
    expected = expected + (NC - 1 + NR - 1)

    sw[...] = swap_matrix()

    for i in range(8):
        loads[i].wait()
        high = surf[:, 16 * i : 16 * (i + 1), :].reshape(256, TY).astype(BF)
        bb[0, pl.ds((8 + 16 * i) * C, 256), 0:TY] = mm(sw[...], high).astype(BF)

    load(w_patch, wp)
    for n, w in enumerate((w_query, w_key, w_value, w_out)):
        load(w, wqkvo.at[n])
    load(w_unpatch, wu)

    strip = jnp.zeros((32, 512), F32)
    for k in range(4):
        strip = strip + mm(
            strip_select(k, TY, 0, TY - 3), bb[0, pl.ds((8 + 32 * k) * C, 512), 0:TY], NT
        )
    strip = strip.astype(BF)
    for l in range(2):
        loads[8 + l].wait()
    cols = jnp.zeros((32, TX), F32)
    rows_c = jnp.zeros((32, TY), F32)
    for l in range(2):
        field = cp[l, 8 : 8 + TX, 0:TY].astype(BF)
        cols = cols + mm(strip_select(l, TY, 0, TY - 3), field, NT)
        rows_c = rows_c + mm(strip_select(l, TX, 0, TX - 3), field)
    cols = cols.astype(BF)
    rows_c = rows_c.astype(BF)
    for side in range(2):
        half = slice(16 * side, 16 * (side + 1))
        col_s[side, :, 0:128] = cols[half]
        col_s[side, :, 128:640] = strip[half]
        col_s[side, :, 640:768] = cols[half]
        row_s[side, 48:64, :] = rows_c[half]
    row_s[0, 0:48, :] = bb[0, 8 * C : 11 * C, 0:TY]
    row_s[1, 0:48, :] = bb[0, (5 + TX) * C : (8 + TX) * C, 0:TY]

    pl.semaphore_wait(barrier, expected)

    lower = pl.ds(0, 256)
    upper = pl.ds(512, 256)
    pieces = (
        (row_s.at[0], row_r.at[1]),
        (row_s.at[1], row_r.at[0]),
        (col_s.at[0], col_r.at[1]),
        (col_s.at[1], col_r.at[0]),
        (col_s.at[0, :, lower], corner_r.at[3]),
        (col_s.at[1, :, lower], corner_r.at[2]),
        (col_s.at[0, :, upper], corner_r.at[1]),
        (col_s.at[1, :, upper], corner_r.at[0]),
    )

    def halo_copy(d):
        src, dst = pieces[d]
        return pltpu.make_async_remote_copy(
            src_ref=src,
            dst_ref=dst,
            send_sem=halo_send.at[d],
            recv_sem=halo_recv.at[OPPOSITE[d]],
            device_id=(row + STEPS[d][0], col + STEPS[d][1]),
            device_id_type=MESH,
        )

    for d in (4, 5, 6, 7, 2, 3, 0, 1):
        @pl.when(has(STEPS[d]))
        def _():
            halo_copy(d).start()

    for i in range(8):
        block = surf[:, 16 * i : 16 * (i + 1), :].reshape(256, TY)
        low = (block - block.astype(BF).astype(F32)).astype(BF)
        rows = pl.ds((8 + 16 * i) * C, 256)
        s_ref[rows, 0:TY] = bb[0, rows, 0:TY].astype(F32) + mm(sw[...], low)

    s_ref[0:80, 0:TY] = jnp.zeros((80, TY), F32)
    s_ref[139 * 16 : U * 16, 0:TY] = jnp.zeros((80, TY), F32)
    bb[0, 0:80, 0:TY] = jnp.zeros((80, TY), BF)
    bb[0, 139 * 16 : U * 16, 0:TY] = jnp.zeros((80, TY), BF)
    bb[1, 0:96, :] = jnp.zeros((96, W), BF)
    bb[1, 138 * 16 : U * 16, :] = jnp.zeros((96, W), BF)
    cp[2, 0:8, :] = jnp.zeros((8, W), F32)
    cp[2, 8 + TX : U, :] = jnp.zeros((8, W), F32)
    cp[2, 8 : 8 + TX, TY:W] = jnp.zeros((TX, 128), F32)

    loads[10].wait()
    loads[11].wait()
    spread = ones_where((iota2((C, DEPTH), 1) & 15) == iota2((C, DEPTH), 0))
    tiled = mm(wst[...].astype(BF), spread)
    band = iota2((C, DEPTH), 1) >> 4
    for l in range(LAYERS):
        for b in range(3):
            pick = [
                tiled[((l * 9 + a * 3 + b) * C) : ((l * 9 + a * 3 + b) * C) + C] for a in range(3)
            ]
            for xo in range(G):
                block = jnp.where(
                    band == xo,
                    pick[0],
                    jnp.where(
                        band == xo + 1, pick[1], jnp.where(band == xo + 2, pick[2], 0.0)
                    ),
                )
                am[l, C * xo : C * (xo + 1), DEPTH * b : DEPTH * (b + 1)] = block.astype(BF)

    loads[12].wait()
    for p in range(PATCH):
        turned = mm(sw[...], wp[:, p, :, :].reshape(256, E))
        wq[:, C * p : C * (p + 1), :] = turned.astype(BF).reshape(PATCH, C, E)
    for n in range(4):
        loads[13 + n].wait()

    for d in range(8):
        @pl.when(has(STEPS[d]))
        def _():
            halo_copy(OPPOSITE[d]).wait_recv()

    for side, u, first in ((0, 5, 5), (1, 8 + TX, 0)):
        halo = row_r[side, 0:48, :]
        s_ref[u * C : (u + 3) * C, 0:TY] = halo.astype(F32)
        bb[0, u * C : (u + 3) * C, 0:TY] = halo
        for l in range(2):
            at = iota2((8, 16), 0) - first
            s = iota2((8, 16), 1) - 4 * l
            pick = ones_where((at == s) & (s >= 0) & (s < 3))
            top = 0 if side == 0 else 8 + TX
            cp[l, top : top + 8, 0:TY] = mm(pick, row_r[side, 48:64, :])
    def place(rows, strip, k):
        columns = mm(strip, strip_place(k), TN)
        s_ref[rows, TY:W] = columns
        bb[0, rows, TY:W] = columns.astype(BF)

    both = jnp.concatenate([col_r[0, :, 128:640], col_r[1, :, 128:640]], axis=0)
    both_c = jnp.concatenate([col_r[0, :, 0:128], col_r[1, :, 0:128]], axis=0)
    for k in range(4):
        place(pl.ds((8 + 32 * k) * C, 512), both, k)
    for l in range(2):
        cp[l, 8 : 8 + TX, TY:W] = mm(both_c, strip_place(l), TN)
    above = jnp.concatenate([corner_r[0], corner_r[1]], axis=0)
    below = jnp.concatenate([corner_r[2], corner_r[3]], axis=0)
    place(pl.ds(0, 128), above[:, 0:128], 3)
    place(pl.ds((8 + TX) * C, 128), below[:, 128:256], 0)
    for l in range(2):
        cp[l, 0:8, TY:W] = mm(above[:, 128:256], strip_place(l), TN)[TX - 8 : TX]
        cp[l, 8 + TX : U, TY:W] = mm(below[:, 0:128], strip_place(l), TN)[0:8]

    def gather(half, d, peer=None):
        first, end = PARTS[half]
        cells = pl.ds(16 * first, 16 * (end - first))
        return pltpu.make_async_remote_copy(
            src_ref=g0.at[0, cells],
            dst_ref=g0.at[d, cells],
            send_sem=gather_send.at[half, d],
            recv_sem=gather_recv.at[half, d],
            device_id=(row, flipped(col_bits, d) if peer is None else peer),
            device_id_type=MESH,
        )

    def shifted(src, u):
        window = bb[src, (u - 1) * C : (u - 1) * C + DEPTH, :]
        return jnp.concatenate(
            [
                jnp.concatenate([window[:, W - 1 :], window[:, : W - 1]], axis=1),
                window,
                jnp.concatenate([window[:, 1:], window[:, :1]], axis=1),
            ],
            axis=0,
        )

    def update(l, u, gain, lanes):
        for x in range(G):
            if u + x > 137 - l:
                continue
            rows = slice((u + x) * C, (u + x + 1) * C)
            new = s_ref[rows, lanes] + cp[l, u + x : u + x + 1, lanes] * (
                gain[C * x : C * (x + 1)]
            )
            s_ref[rows, lanes] = new
            bb[(l + 1) % 2, rows, lanes] = new.astype(BF)

    def advance(l, pair):
        starts = [6 + l + G * (2 * pair + n) for n in range(2)]
        windows = [shifted(l % 2, u) for u in starts]
        for u, window in zip(starts, windows):
            update(l, u, jnp.tanh(mm(am[l], window[:, :TY])), slice(0, TY))
        if l < LAYERS - 1:
            edges = jnp.tanh(
                mm(am[l], jnp.concatenate([window[:, TY:] for window in windows], axis=1))
            )
            for n, u in enumerate(starts):
                update(l, u, edges[:, 128 * n : 128 * (n + 1)], slice(TY, W))

    last = LAYERS % 2

    def patch(half):
        first, end = PARTS[half]
        count = 16 * (end - first)
        for i in range(first, end):
            block = bb[last, pl.ds((8 + 16 * i) * C, 256), 0:TY]
            zt[i] = mm(sw[...], block, NT).astype(BF)
        part = jnp.zeros((count, E), F32)
        for q in range(PATCH):
            block = zt[first:end, 16 * q : 16 * (q + 1), :]
            part = part + mm(block.reshape(count, 256), wq[q])
        g0[0, 16 * first : 16 * end, :] = normed(part)
        for target in range(NC):
            @pl.when(col != target)
            def _():
                gather(half, flipped(col_bits, target), target).start()

        return part

    parts = []
    for step in range(11 + 2 * (LAYERS - 1)):
        for l in range(LAYERS):
            pair = step - 2 * l
            if 0 <= pair < 11:
                advance(l, pair)
                if l == LAYERS - 1 and pair == 3:
                    parts.append(patch(0))
    parts.append(patch(1))
    coarse = jnp.concatenate(parts, axis=0)

    def a2a(phase, src, dst, d):
        rows = pl.ds(16 * d, 16)
        return pltpu.make_async_remote_copy(
            src_ref=src.at[rows],
            dst_ref=dst.at[rows],
            send_sem=a2a_send.at[phase, d],
            recv_sem=a2a_recv.at[phase],
            device_id=(flipped(row_bits, d), col),
            device_id_type=MESH,
        )

    def exchange(phase, src, dst, meanwhile):
        for d in ROW_ORDER:
            a2a(phase, src, dst, d).start()
        dst[0:16, :] = src[0:16, :]
        meanwhile()
        rest = pl.ds(16, 16 * (NR - 1))
        pltpu.make_async_remote_copy(
            src_ref=src.at[rest],
            dst_ref=dst.at[rest],
            send_sem=a2a_send.at[phase, 1],
            recv_sem=a2a_recv.at[phase],
            device_id=(flipped(row_bits, 1), col),
            device_id_type=MESH,
        ).wait_recv()

    def state_back():
        for i in range(8):
            block = s_ref[pl.ds((8 + 16 * i) * C, 256), 0:TY]
            high = block.astype(BF)
            low = (block - high.astype(F32)).astype(BF)
            turned = mm(sw[...], high) + mm(sw[...], low)
            state[:, 16 * i : 16 * (i + 1), :] = turned.reshape(C, 16, TY)

    def unpatch_weights():
        one = ones_where(iota2((E, E), 0) == iota2((E, E), 1))
        wkt[...] = mm(wqkvo[1, 1], one, TN).astype(BF)
        loads[17].wait()
        for c in range(C):
            turned = mm(sw[...], wu[:, 256 * c : 256 * (c + 1)], NT).astype(BF)
            wq[:, C * c : C * (c + 1), :] = turned.reshape(PATCH, C, E)

    def before_columns():
        state_back()
        unpatch_weights()

    def before_unpatch():
        one = ones_where(iota2((E, E), 0) == iota2((E, E), 1))
        for q in range(PATCH):
            wq[q] = mm(wq[q], one, TN).astype(BF)

    head = iota2((16, E), 1) >> 5
    queries = mm(g0[0], wqkvo[0, 0])
    mixed = []
    for half in range(2):
        first, end = PARTS[half]
        cells = slice(16 * first, 16 * end)
        for d in (0,) + GATHER_ORDER:
            if d > 0:
                gather(half, d).wait_recv()
            k0[d, cells, :] = mm(g0[d, cells, :], wqkvo[1, 0]).astype(BF)
            v0[d, cells, :] = mm(g0[d, cells, :], wqkvo[2, 0]).astype(BF)
        for i in range(first, end):
            rows = slice(16 * i, 16 * (i + 1))
            query_set = jnp.concatenate(
                [jnp.where(head == h, queries[rows], 0.0).astype(BF) for h in range(H)], axis=0
            )
            powers = powers_of(mm(query_set, k0[:, rows, :].reshape(128, E), NT))
            whole = mm(powers, v0[:, rows, :].reshape(128, E))
            total = mm(powers, jnp.ones((128, E), BF))
            mixed.append(own_lanes(head, whole) / own_lanes(head, total))
    coarse = coarse + mm(jnp.concatenate(mixed, axis=0).astype(BF), wqkvo[3, 0])

    r = iota2((CELLS, CELLS), 0)
    k = iota2((CELLS, CELLS), 1)
    turn = ones_where(k == (r & 7) * 16 + ((r >> 3) ^ row))
    n1[...] = packed(mm(turn, normed(coarse)))
    exchange(0, n1, g1, before_columns)
    mix1[...] = packed(
        attend(unpacked(g1[...]).astype(BF), wqkvo[0, 1], wkt[...], wqkvo[2, 1])
    )
    exchange(1, mix1, m1, before_unpatch)
    back = mm(turn, unpacked(m1[...]).astype(BF), TN).astype(BF)
    coarse = coarse + mm(back, wqkvo[3, 1])
    coarse = coarse.astype(BF)
    for q in range(PATCH):
        cells = mm(coarse, wq[q]).astype(BF)
        zt[:, 16 * q : 16 * (q + 1), :] = cells.reshape(8, 16, 256)
    for d in range(8):
        @pl.when(has(STEPS[d]))
        def _():
            halo_copy(d).wait_send()

    for half in range(2):
        for d in COL_ORDER:
            gather(half, d).wait_send()
    for d in ROW_ORDER:
        a2a(0, n1, g1, d).wait_send()
        a2a(1, mix1, m1, d).wait_send()


def add_kernel(zt, state, out, swap, held, store_sem):
    swap[...] = swap_matrix()
    stores = []
    for i in range(8):
        rows = slice(16 * i, 16 * (i + 1))
        detail = mm(zt[i], swap[...], TN)
        held[:, rows, :] = state[:, rows, :] + detail.reshape(C, 16, TY)
        copy = pltpu.make_async_copy(held.at[:, rows, :], out.at[:, rows, :], store_sem.at[i])
        copy.start()
        stores.append(copy)
    for copy in stores:
        copy.wait()


def on_device(surface, coupling, w_stencil, w_patch, w_query, w_key, w_value, w_out, w_unpatch):
    anywhere = pl.BlockSpec(memory_space=pl.ANY)
    in_vmem = pl.BlockSpec(memory_space=pltpu.VMEM)
    state, cells = pl.pallas_call(
        main_kernel,
        out_shape=(pltpu.VMEM((C, TX, TY), F32), pltpu.VMEM((8, 256, 256), BF)),
        in_specs=[anywhere] * 9,
        out_specs=(in_vmem, in_vmem),
        scratch_shapes=[
            pltpu.VMEM((C, TX, TY), F32),
            pltpu.VMEM((LAYERS, U, W), F32),
            pltpu.VMEM((LAYERS * 9 * C, C), F32),
            pltpu.VMEM((C, PATCH, PATCH, E), BF),
            pltpu.VMEM((E, C * 256), BF),
            pltpu.VMEM((PATCH, 256, E), BF),
            pltpu.VMEM((4, 2, E, E), BF),
            pltpu.VMEM((E, E), BF),
            pltpu.VMEM((256, 256), BF),
            pltpu.VMEM((LAYERS, G * C, 3 * DEPTH), BF),
            pltpu.VMEM((U * C, W), F32),
            pltpu.VMEM((2, U * C, W), BF),
            pltpu.VMEM((2, 64, TY), BF),
            pltpu.VMEM((2, 16, 768), BF),
            pltpu.VMEM((2, 64, TY), BF),
            pltpu.VMEM((2, 16, 768), BF),
            pltpu.VMEM((4, 16, 256), BF),
            pltpu.VMEM((NC, CELLS, E), BF),
            pltpu.VMEM((NC, CELLS, E), BF),
            pltpu.VMEM((NC, CELLS, E), BF),
            pltpu.VMEM((256, 128), BF),
            pltpu.VMEM((256, 128), BF),
            pltpu.VMEM((256, 128), BF),
            pltpu.VMEM((256, 128), BF),
            pltpu.SemaphoreType.DMA((18,)),
            pltpu.SemaphoreType.DMA((8,)),
            pltpu.SemaphoreType.DMA((8,)),
            pltpu.SemaphoreType.DMA((2, NC)),
            pltpu.SemaphoreType.DMA((2, NC)),
            pltpu.SemaphoreType.DMA((2, NR)),
            pltpu.SemaphoreType.DMA((2,)),
        ],
        compiler_params=pltpu.CompilerParams(
            collective_id=0, has_side_effects=True, vmem_limit_bytes=60 * 1024 * 1024
        ),
    )(
        surface,
        coupling,
        w_stencil.reshape(LAYERS * 9 * C, C),
        w_patch.reshape(C, PATCH, PATCH, E),
        w_query,
        w_key,
        w_value,
        w_out,
        w_unpatch,
    )
    return pl.pallas_call(
        add_kernel,
        out_shape=jax.ShapeDtypeStruct((C, TX, TY), F32),
        in_specs=[in_vmem, in_vmem],
        out_specs=anywhere,
        scratch_shapes=[
            pltpu.VMEM((256, 256), BF),
            pltpu.VMEM((C, TX, TY), F32),
            pltpu.SemaphoreType.DMA((8,)),
        ],
        compiler_params=pltpu.CompilerParams(vmem_limit_bytes=32 * 1024 * 1024),
    )(cells, state)


def solution(mesh):
    in_specs = (P(None, "row", "col"), P(None, "row", "col"), P(), P(), P(), P(), P(), P(), P())
    out_specs = P(None, "row", "col")
    return jax.shard_map(
        on_device, mesh=mesh, in_specs=in_specs, out_specs=out_specs, check_vma=False
    )
```

```python
import jax
import jax.numpy as jnp
from jax import lax
from jax.experimental import pallas as pl
from jax.experimental.pallas import tpu as pltpu
from jax.sharding import PartitionSpec as P

C = 16
E = 256
H = 8
PATCH = 16
LAYERS = 3
NR = 16
NC = 8
TX = 128
TY = 256
CELLS = 128
U = TX + 16
W = TY + 128
G = 6
DEPTH = (G + 2) * C
BF = jnp.bfloat16
F32 = jnp.float32
MESH = pl.DeviceIdType.MESH
NT = (((1,), (1,)), ((), ()))
TN = (((0,), (0,)), ((), ()))

STEPS = ((-1, 0), (1, 0), (0, -1), (0, 1), (-1, -1), (-1, 1), (1, -1), (1, 1))
OPPOSITE = (1, 0, 3, 2, 7, 6, 5, 4)
ROW_ORDER = (10, 11, 8, 9, 14, 15, 12, 13, 6, 7, 4, 5, 2, 3, 1)
COL_ORDER = (6, 5, 7, 2, 4, 1, 3)
GATHER_ORDER = (2, 1, 3, 4, 6, 5, 7)
PARTS = ((0, 2), (2, 8))


def iota2(shape, dim):
    return lax.broadcasted_iota(jnp.int32, shape, dim)


def ones_where(mask):
    return jnp.where(mask, 1.0, 0.0).astype(BF)


def swap_matrix():
    row = iota2((256, 256), 0)
    col = iota2((256, 256), 1)
    return ones_where(col == (row & 15) * 16 + (row >> 4))


def mm(a, b, dims=None):
    if dims is None:
        return jnp.dot(a, b, preferred_element_type=F32)
    return lax.dot_general(a, b, dims, preferred_element_type=F32)


def strip_select(k, size, near, far):
    row = iota2((32, size), 0)
    at = iota2((32, size), 1)
    s = (row & 15) - 4 * k
    goal = jnp.where(row < 16, near, far) + s
    return ones_where((s >= 0) & (s < 3) & (at == goal))


def strip_place(k):
    return strip_select(k, 128, 125, 0)


def normed(coarse):
    mean = jnp.mean(coarse * coarse, axis=-1, keepdims=True)
    return (coarse * lax.rsqrt(mean + 1e-06)).astype(BF)


def powers_of(scores):
    scores = scores * (E // H) ** (-0.5)
    return jnp.exp(scores - jnp.max(scores, axis=-1, keepdims=True)).astype(BF)


def flipped(bits, d):
    return sum(((1 - bit) if (d >> n) & 1 else bit) * (1 << n) for n, bit in enumerate(bits))


def packed(cells):
    parts = cells.reshape(16, 8, E)
    return (
        jnp.stack([parts[:, :, :128], parts[:, :, 128:]], axis=1).reshape(256, 128).astype(BF)
    )


def unpacked(rows):
    parts = rows.astype(F32).reshape(16, 2, 8, 128)
    return jnp.concatenate([parts[:, 0], parts[:, 1]], axis=-1).reshape(CELLS, E)


def own_lanes(head, stacked):
    return sum(jnp.where(head == h, stacked[16 * h : 16 * (h + 1)], 0.0) for h in range(H))


def attend(cells, w_q, w_k_turned, w_v):
    queries = mm(cells, w_q).astype(BF)
    lookups = mm(w_k_turned, cells, NT)
    values = mm(cells, w_v)
    head = iota2((128, E), 1) >> 5
    channel_head = iota2((E, 128), 0) >> 5
    lookup_set = jnp.concatenate(
        [jnp.where(channel_head == h, lookups, 0.0).astype(BF) for h in range(H)], axis=1
    )
    scores = mm(queries, lookup_set)
    powers = jnp.concatenate(
        [powers_of(scores[:, 128 * h : 128 * (h + 1)]) for h in range(H)], axis=1
    )
    value_set = jnp.concatenate(
        [jnp.where(head == h, values, 0.0).astype(BF) for h in range(H)], axis=0
    )
    own_head = jnp.concatenate([ones_where(head == h) for h in range(H)], axis=0)
    return mm(powers, value_set) / mm(powers, own_head)


def main_kernel(
    surface, coupling, w_stencil, w_patch, w_query, w_key, w_value, w_out, w_unpatch,
    state, zt,
    surf, cp, wst, wp, wu, wq, wqkvo, wkt, sw, am, s_ref, bb,
    row_s, col_s, row_r, col_r, corner_r,
    g0, k0, v0, n1, g1, mix1, m1,
    load_sem, halo_send, halo_recv, gather_send, gather_recv, a2a_send, a2a_recv,
):
    row = lax.axis_index("row")
    col = lax.axis_index("col")
    row_bits = [lax.rem(lax.div(row, 1 << n), 2) for n in range(4)]
    col_bits = [lax.rem(lax.div(col, 1 << n), 2) for n in range(3)]

    row_r[...] = jnp.zeros_like(row_r)
    col_r[...] = jnp.zeros_like(col_r)
    corner_r[...] = jnp.zeros_like(corner_r)

    def has(step):
        dr, dc = step
        ok = row >= 0
        if dr < 0:
            ok = row > 0
        if dr > 0:
            ok = row < NR - 1
        if dc < 0:
            ok = ok & (col > 0)
        if dc > 0:
            ok = ok & (col < NC - 1)
        return ok

    barrier = pltpu.get_barrier_semaphore()
    expected = jnp.int32(0)
    for step in STEPS[4:] + STEPS[:4]:
        @pl.when(has(step))
        def _():
            pl.semaphore_signal(
                barrier, inc=1, device_id=(row + step[0], col + step[1]), device_id_type=MESH
            )

        expected = expected + jnp.where(has(step), 1, 0)
    loads = []

    def load(src, dst):
        copy = pltpu.make_async_copy(src, dst, load_sem.at[len(loads)])
        copy.start()
        loads.append(copy)

    for i in range(8):
        load(surface.at[:, pl.ds(16 * i, 16), :], surf.at[:, pl.ds(16 * i, 16), :])
    for l in range(LAYERS):
        load(coupling.at[l], cp.at[l, pl.ds(8, TX), pl.ds(0, TY)])
    load(w_stencil, wst)

    for d in COL_ORDER:
        pl.semaphore_signal(
            barrier, inc=1, device_id=(row, flipped(col_bits, d)), device_id_type=MESH
        )
    for d in ROW_ORDER:
        pl.semaphore_signal(
            barrier, inc=1, device_id=(flipped(row_bits, d), col), device_id_type=MESH
        )
    expected = expected + (NC - 1 + NR - 1)

    sw[...] = swap_matrix()

    for i in range(8):
        loads[i].wait()
        high = surf[:, 16 * i : 16 * (i + 1), :].reshape(256, TY).astype(BF)
        bb[0, pl.ds((8 + 16 * i) * C, 256), 0:TY] = mm(sw[...], high).astype(BF)

    load(w_patch, wp)
    for n, w in enumerate((w_query, w_key, w_value, w_out)):
        load(w, wqkvo.at[n])
    load(w_unpatch, wu)

    strip = jnp.zeros((32, 512), F32)
    for k in range(4):
        strip = strip + mm(
            strip_select(k, TY, 0, TY - 3), bb[0, pl.ds((8 + 32 * k) * C, 512), 0:TY], NT
        )
    strip = strip.astype(BF)
    for l in range(2):
        loads[8 + l].wait()
    cols = jnp.zeros((32, TX), F32)
    rows_c = jnp.zeros((32, TY), F32)
    for l in range(2):
        field = cp[l, 8 : 8 + TX, 0:TY].astype(BF)
        cols = cols + mm(strip_select(l, TY, 0, TY - 3), field, NT)
        rows_c = rows_c + mm(strip_select(l, TX, 0, TX - 3), field)
    cols = cols.astype(BF)
    rows_c = rows_c.astype(BF)
    for side in range(2):
        half = slice(16 * side, 16 * (side + 1))
        col_s[side, :, 0:128] = cols[half]
        col_s[side, :, 128:640] = strip[half]
        col_s[side, :, 640:768] = cols[half]
        row_s[side, 48:64, :] = rows_c[half]
    row_s[0, 0:48, :] = bb[0, 8 * C : 11 * C, 0:TY]
    row_s[1, 0:48, :] = bb[0, (5 + TX) * C : (8 + TX) * C, 0:TY]

    pl.semaphore_wait(barrier, expected)

    lower = pl.ds(0, 256)
    upper = pl.ds(512, 256)
    pieces = (
        (row_s.at[0], row_r.at[1]),
        (row_s.at[1], row_r.at[0]),
        (col_s.at[0], col_r.at[1]),
        (col_s.at[1], col_r.at[0]),
        (col_s.at[0, :, lower], corner_r.at[3]),
        (col_s.at[1, :, lower], corner_r.at[2]),
        (col_s.at[0, :, upper], corner_r.at[1]),
        (col_s.at[1, :, upper], corner_r.at[0]),
    )

    def halo_copy(d):
        src, dst = pieces[d]
        return pltpu.make_async_remote_copy(
            src_ref=src,
            dst_ref=dst,
            send_sem=halo_send.at[d],
            recv_sem=halo_recv.at[OPPOSITE[d]],
            device_id=(row + STEPS[d][0], col + STEPS[d][1]),
            device_id_type=MESH,
        )

    for d in (4, 5, 6, 7, 2, 3, 0, 1):
        @pl.when(has(STEPS[d]))
        def _():
            halo_copy(d).start()

    for i in range(8):
        block = surf[:, 16 * i : 16 * (i + 1), :].reshape(256, TY)
        low = (block - block.astype(BF).astype(F32)).astype(BF)
        rows = pl.ds((8 + 16 * i) * C, 256)
        s_ref[rows, 0:TY] = bb[0, rows, 0:TY].astype(F32) + mm(sw[...], low)

    s_ref[0:80, 0:TY] = jnp.zeros((80, TY), F32)
    s_ref[139 * 16 : U * 16, 0:TY] = jnp.zeros((80, TY), F32)
    bb[0, 0:80, 0:TY] = jnp.zeros((80, TY), BF)
    bb[0, 139 * 16 : U * 16, 0:TY] = jnp.zeros((80, TY), BF)
    bb[1, 0:96, :] = jnp.zeros((96, W), BF)
    bb[1, 138 * 16 : U * 16, :] = jnp.zeros((96, W), BF)
    cp[2, 0:8, :] = jnp.zeros((8, W), F32)
    cp[2, 8 + TX : U, :] = jnp.zeros((8, W), F32)
    cp[2, 8 : 8 + TX, TY:W] = jnp.zeros((TX, 128), F32)

    loads[10].wait()
    loads[11].wait()
    spread = ones_where((iota2((C, DEPTH), 1) & 15) == iota2((C, DEPTH), 0))
    tiled = mm(wst[...].astype(BF), spread)
    band = iota2((C, DEPTH), 1) >> 4
    for l in range(LAYERS):
        for b in range(3):
            pick = [
                tiled[((l * 9 + a * 3 + b) * C) : ((l * 9 + a * 3 + b) * C) + C] for a in range(3)
            ]
            for xo in range(G):
                block = jnp.where(
                    band == xo,
                    pick[0],
                    jnp.where(
                        band == xo + 1, pick[1], jnp.where(band == xo + 2, pick[2], 0.0)
                    ),
                )
                am[l, C * xo : C * (xo + 1), DEPTH * b : DEPTH * (b + 1)] = block.astype(BF)

    loads[12].wait()
    for p in range(PATCH):
        turned = mm(sw[...], wp[:, p, :, :].reshape(256, E))
        wq[:, C * p : C * (p + 1), :] = turned.astype(BF).reshape(PATCH, C, E)
    for n in range(4):
        loads[13 + n].wait()

    for d in range(8):
        @pl.when(has(STEPS[d]))
        def _():
            halo_copy(OPPOSITE[d]).wait_recv()

    for side, u, first in ((0, 5, 5), (1, 8 + TX, 0)):
        halo = row_r[side, 0:48, :]
        s_ref[u * C : (u + 3) * C, 0:TY] = halo.astype(F32)
        bb[0, u * C : (u + 3) * C, 0:TY] = halo
        for l in range(2):
            at = iota2((8, 16), 0) - first
            s = iota2((8, 16), 1) - 4 * l
            pick = ones_where((at == s) & (s >= 0) & (s < 3))
            top = 0 if side == 0 else 8 + TX
            cp[l, top : top + 8, 0:TY] = mm(pick, row_r[side, 48:64, :])
    def place(rows, strip, k):
        columns = mm(strip, strip_place(k), TN)
        s_ref[rows, TY:W] = columns
        bb[0, rows, TY:W] = columns.astype(BF)

    both = jnp.concatenate([col_r[0, :, 128:640], col_r[1, :, 128:640]], axis=0)
    both_c = jnp.concatenate([col_r[0, :, 0:128], col_r[1, :, 0:128]], axis=0)
    for k in range(4):
        place(pl.ds((8 + 32 * k) * C, 512), both, k)
    for l in range(2):
        cp[l, 8 : 8 + TX, TY:W] = mm(both_c, strip_place(l), TN)
    above = jnp.concatenate([corner_r[0], corner_r[1]], axis=0)
    below = jnp.concatenate([corner_r[2], corner_r[3]], axis=0)
    place(pl.ds(0, 128), above[:, 0:128], 3)
    place(pl.ds((8 + TX) * C, 128), below[:, 128:256], 0)
    for l in range(2):
        cp[l, 0:8, TY:W] = mm(above[:, 128:256], strip_place(l), TN)[TX - 8 : TX]
        cp[l, 8 + TX : U, TY:W] = mm(below[:, 0:128], strip_place(l), TN)[0:8]

    def gather(half, d, peer=None):
        first, end = PARTS[half]
        cells = pl.ds(16 * first, 16 * (end - first))
        return pltpu.make_async_remote_copy(
            src_ref=g0.at[0, cells],
            dst_ref=g0.at[d, cells],
            send_sem=gather_send.at[half, d],
            recv_sem=gather_recv.at[half, d],
            device_id=(row, flipped(col_bits, d) if peer is None else peer),
            device_id_type=MESH,
        )

    def shifted(src, u):
        window = bb[src, (u - 1) * C : (u - 1) * C + DEPTH, :]
        return jnp.concatenate(
            [
                jnp.concatenate([window[:, W - 1 :], window[:, : W - 1]], axis=1),
                window,
                jnp.concatenate([window[:, 1:], window[:, :1]], axis=1),
            ],
            axis=0,
        )

    def update(l, u, gain, lanes):
        for x in range(G):
            if u + x > 137 - l:
                continue
            rows = slice((u + x) * C, (u + x + 1) * C)
            new = s_ref[rows, lanes] + cp[l, u + x : u + x + 1, lanes] * (
                gain[C * x : C * (x + 1)]
            )
            s_ref[rows, lanes] = new
            bb[(l + 1) % 2, rows, lanes] = new.astype(BF)

    def advance(l, pair):
        starts = [6 + l + G * (2 * pair + n) for n in range(2)]
        windows = [shifted(l % 2, u) for u in starts]
        for u, window in zip(starts, windows):
            update(l, u, jnp.tanh(mm(am[l], window[:, :TY])), slice(0, TY))
        if l < LAYERS - 1:
            edges = jnp.tanh(
                mm(am[l], jnp.concatenate([window[:, TY:] for window in windows], axis=1))
            )
            for n, u in enumerate(starts):
                update(l, u, edges[:, 128 * n : 128 * (n + 1)], slice(TY, W))

    last = LAYERS % 2

    def patch(half):
        first, end = PARTS[half]
        count = 16 * (end - first)
        for i in range(first, end):
            block = bb[last, pl.ds((8 + 16 * i) * C, 256), 0:TY]
            zt[i] = mm(sw[...], block, NT).astype(BF)
        part = jnp.zeros((count, E), F32)
        for q in range(PATCH):
            block = zt[first:end, 16 * q : 16 * (q + 1), :]
            part = part + mm(block.reshape(count, 256), wq[q])
        g0[0, 16 * first : 16 * end, :] = normed(part)
        for target in range(NC):
            @pl.when(col != target)
            def _():
                gather(half, flipped(col_bits, target), target).start()

        return part

    parts = []
    for step in range(11 + 2 * (LAYERS - 1)):
        for l in range(LAYERS):
            pair = step - 2 * l
            if 0 <= pair < 11:
                advance(l, pair)
                if l == LAYERS - 1 and pair == 2:
                    parts.append(patch(0))
    parts.append(patch(1))
    coarse = jnp.concatenate(parts, axis=0)

    def a2a(phase, src, dst, d):
        rows = pl.ds(16 * d, 16)
        return pltpu.make_async_remote_copy(
            src_ref=src.at[rows],
            dst_ref=dst.at[rows],
            send_sem=a2a_send.at[phase, d],
            recv_sem=a2a_recv.at[phase],
            device_id=(flipped(row_bits, d), col),
            device_id_type=MESH,
        )

    def exchange(phase, src, dst, meanwhile):
        for d in ROW_ORDER:
            a2a(phase, src, dst, d).start()
        dst[0:16, :] = src[0:16, :]
        meanwhile()
        rest = pl.ds(16, 16 * (NR - 1))
        pltpu.make_async_remote_copy(
            src_ref=src.at[rest],
            dst_ref=dst.at[rest],
            send_sem=a2a_send.at[phase, 1],
            recv_sem=a2a_recv.at[phase],
            device_id=(flipped(row_bits, 1), col),
            device_id_type=MESH,
        ).wait_recv()

    def state_back():
        for i in range(8):
            block = s_ref[pl.ds((8 + 16 * i) * C, 256), 0:TY]
            high = block.astype(BF)
            low = (block - high.astype(F32)).astype(BF)
            turned = mm(sw[...], high) + mm(sw[...], low)
            state[:, 16 * i : 16 * (i + 1), :] = turned.reshape(C, 16, TY)

    def unpatch_weights():
        one = ones_where(iota2((E, E), 0) == iota2((E, E), 1))
        wkt[...] = mm(wqkvo[1, 1], one, TN).astype(BF)
        loads[17].wait()
        for c in range(C):
            turned = mm(sw[...], wu[:, 256 * c : 256 * (c + 1)], NT).astype(BF)
            wq[:, C * c : C * (c + 1), :] = turned.reshape(PATCH, C, E)

    def before_columns():
        state_back()
        unpatch_weights()

    def before_unpatch():
        one = ones_where(iota2((E, E), 0) == iota2((E, E), 1))
        for q in range(PATCH):
            wq[q] = mm(wq[q], one, TN).astype(BF)

    head = iota2((16, E), 1) >> 5
    queries = mm(g0[0], wqkvo[0, 0])
    mixed = []
    for half in range(2):
        first, end = PARTS[half]
        cells = slice(16 * first, 16 * end)
        for d in (0,) + GATHER_ORDER:
            if d > 0:
                gather(half, d).wait_recv()
            k0[d, cells, :] = mm(g0[d, cells, :], wqkvo[1, 0]).astype(BF)
            v0[d, cells, :] = mm(g0[d, cells, :], wqkvo[2, 0]).astype(BF)
        for i in range(first, end):
            rows = slice(16 * i, 16 * (i + 1))
            query_set = jnp.concatenate(
                [jnp.where(head == h, queries[rows], 0.0).astype(BF) for h in range(H)], axis=0
            )
            powers = powers_of(mm(query_set, k0[:, rows, :].reshape(128, E), NT))
            whole = mm(powers, v0[:, rows, :].reshape(128, E))
            total = mm(powers, jnp.ones((128, E), BF))
            mixed.append(own_lanes(head, whole) / own_lanes(head, total))
    coarse = coarse + mm(jnp.concatenate(mixed, axis=0).astype(BF), wqkvo[3, 0])

    r = iota2((CELLS, CELLS), 0)
    k = iota2((CELLS, CELLS), 1)
    turn = ones_where(k == (r & 7) * 16 + ((r >> 3) ^ row))
    n1[...] = packed(mm(turn, normed(coarse)))
    exchange(0, n1, g1, before_columns)
    mix1[...] = packed(
        attend(unpacked(g1[...]).astype(BF), wqkvo[0, 1], wkt[...], wqkvo[2, 1])
    )
    exchange(1, mix1, m1, before_unpatch)
    back = mm(turn, unpacked(m1[...]).astype(BF), TN).astype(BF)
    coarse = coarse + mm(back, wqkvo[3, 1])
    coarse = coarse.astype(BF)
    for q in range(PATCH):
        cells = mm(coarse, wq[q]).astype(BF)
        zt[:, 16 * q : 16 * (q + 1), :] = cells.reshape(8, 16, 256)
    for d in range(8):
        @pl.when(has(STEPS[d]))
        def _():
            halo_copy(d).wait_send()

    for half in range(2):
        for d in COL_ORDER:
            gather(half, d).wait_send()
    for d in ROW_ORDER:
        a2a(0, n1, g1, d).wait_send()
        a2a(1, mix1, m1, d).wait_send()


def add_kernel(zt, state, out, swap, held, store_sem):
    swap[...] = swap_matrix()
    stores = []
    for i in range(8):
        rows = slice(16 * i, 16 * (i + 1))
        detail = mm(zt[i], swap[...], TN)
        held[:, rows, :] = state[:, rows, :] + detail.reshape(C, 16, TY)
        copy = pltpu.make_async_copy(held.at[:, rows, :], out.at[:, rows, :], store_sem.at[i])
        copy.start()
        stores.append(copy)
    for copy in stores:
        copy.wait()


def on_device(surface, coupling, w_stencil, w_patch, w_query, w_key, w_value, w_out, w_unpatch):
    anywhere = pl.BlockSpec(memory_space=pl.ANY)
    in_vmem = pl.BlockSpec(memory_space=pltpu.VMEM)
    state, cells = pl.pallas_call(
        main_kernel,
        out_shape=(pltpu.VMEM((C, TX, TY), F32), pltpu.VMEM((8, 256, 256), BF)),
        in_specs=[anywhere] * 9,
        out_specs=(in_vmem, in_vmem),
        scratch_shapes=[
            pltpu.VMEM((C, TX, TY), F32),
            pltpu.VMEM((LAYERS, U, W), F32),
            pltpu.VMEM((LAYERS * 9 * C, C), F32),
            pltpu.VMEM((C, PATCH, PATCH, E), BF),
            pltpu.VMEM((E, C * 256), BF),
            pltpu.VMEM((PATCH, 256, E), BF),
            pltpu.VMEM((4, 2, E, E), BF),
            pltpu.VMEM((E, E), BF),
            pltpu.VMEM((256, 256), BF),
            pltpu.VMEM((LAYERS, G * C, 3 * DEPTH), BF),
            pltpu.VMEM((U * C, W), F32),
            pltpu.VMEM((2, U * C, W), BF),
            pltpu.VMEM((2, 64, TY), BF),
            pltpu.VMEM((2, 16, 768), BF),
            pltpu.VMEM((2, 64, TY), BF),
            pltpu.VMEM((2, 16, 768), BF),
            pltpu.VMEM((4, 16, 256), BF),
            pltpu.VMEM((NC, CELLS, E), BF),
            pltpu.VMEM((NC, CELLS, E), BF),
            pltpu.VMEM((NC, CELLS, E), BF),
            pltpu.VMEM((256, 128), BF),
            pltpu.VMEM((256, 128), BF),
            pltpu.VMEM((256, 128), BF),
            pltpu.VMEM((256, 128), BF),
            pltpu.SemaphoreType.DMA((18,)),
            pltpu.SemaphoreType.DMA((8,)),
            pltpu.SemaphoreType.DMA((8,)),
            pltpu.SemaphoreType.DMA((2, NC)),
            pltpu.SemaphoreType.DMA((2, NC)),
            pltpu.SemaphoreType.DMA((2, NR)),
            pltpu.SemaphoreType.DMA((2,)),
        ],
        compiler_params=pltpu.CompilerParams(
            collective_id=0, has_side_effects=True, vmem_limit_bytes=60 * 1024 * 1024
        ),
    )(
        surface,
        coupling,
        w_stencil.reshape(LAYERS * 9 * C, C),
        w_patch.reshape(C, PATCH, PATCH, E),
        w_query,
        w_key,
        w_value,
        w_out,
        w_unpatch,
    )
    return pl.pallas_call(
        add_kernel,
        out_shape=jax.ShapeDtypeStruct((C, TX, TY), F32),
        in_specs=[in_vmem, in_vmem],
        out_specs=anywhere,
        scratch_shapes=[
            pltpu.VMEM((256, 256), BF),
            pltpu.VMEM((C, TX, TY), F32),
            pltpu.SemaphoreType.DMA((8,)),
        ],
        compiler_params=pltpu.CompilerParams(vmem_limit_bytes=32 * 1024 * 1024),
    )(cells, state)


def solution(mesh):
    in_specs = (P(None, "row", "col"), P(None, "row", "col"), P(), P(), P(), P(), P(), P(), P())
    out_specs = P(None, "row", "col")
    return jax.shard_map(
        on_device, mesh=mesh, in_specs=in_specs, out_specs=out_specs, check_vma=False
    )
```
